32 devices in a mesh: blk: 8 (over y, x, core), group: 4 (over z).
Axes of the slice: x: 2, y: 2, z: 4, core: 2. Of those that a mesh axis runs over, the one named last changes fastest.
Arguments:
- row_factors: float32 [16384, 256], P(('blk', 'group')), may hold values from -0.45 to 0.45
- col_factors: float32 [16384, 256], P(('blk', 'group')), may hold values from -0.45 to 0.45
- tile_values: bfloat16 [5, 256, 128, 128], P(None, ('blk', 'group')), may hold values from -4 to 4
- tile_coords: int32 [5, 256, 2], P(None, ('blk', 'group')), may hold values from 0 to 3, as said below
- tile_counts: int32 [5, 32], P(None, ('blk', 'group')), may hold values from 2 to 8, as said below
Outputs:
- rows_out: float32 [16384, 256], P(('blk', 'group'))
- cols_out: float32 [16384, 256], P(('blk', 'group'))
The draws below stay inside these ranges and needn't reach their ends.
Inputs may be any that keep to these rules, and one draw needn't show every extreme that they name: `tile_coords`: the 8 entries of one device and stratum name distinct tiles; the row tile is below 4, the column tile below 4. `tile_counts`: in every stratum some device lists 8 live tiles.
All inputs are finite; a program needn't handle non-finite values.
Results may differ from the reference program's by a relative error of at most 0.005.
Values sent between devices are 32-bit elements; how exact they have to be, the bound alone decides.
No kernel may reach another device: no remote copies, remote signals or barrier semaphores. Data moves between devices by JAX's collectives and lax.ppermute only.
A program may use at most 64 MiB of HBM per device.

```python
import jax
import jax.numpy as jnp
from jax import lax

RANK = 256
TILE = 128
ROW_DEV = 512
COL_BLK = 512
MOST = 8
STRATA = 5
ROWS = 16384
COLS = 16384
N_BLK = 8
N_GROUP = 4
DEVICES = 32


def factor_field(key, count):
    values = 0.15 * jax.random.normal(jax.random.fold_in(key, 3), (count, RANK), jnp.float32)
    return jnp.clip(values, -0.45, 0.45)


def draw_row_factors(key, part):
    return factor_field(jax.random.fold_in(key, 11), ROWS)


def draw_col_factors(key, part):
    return factor_field(jax.random.fold_in(key, 13), COLS)


def draw_tile_coords(key, part):
    col_tiles = COL_BLK // TILE
    places = ROW_DEV // TILE * col_tiles
    scores = jax.random.randint(key, (STRATA, DEVICES, places), 0, 1 << 20) * places + jnp.arange(places)
    ordering = jnp.argsort(scores, axis=-1, stable=True)[:, :, :MOST].astype(jnp.int32)
    stacked = jnp.stack([ordering // col_tiles, ordering % col_tiles], axis=-1)
    return stacked.reshape(STRATA, DEVICES * MOST, 2).astype(jnp.int32)


def draw_tile_counts(key, part):
    counts = jax.random.randint(key, (STRATA, DEVICES), max(1, MOST // 4), MOST + 1)
    busiest = (jnp.arange(STRATA) * 97 + 5) % DEVICES
    return counts.at[jnp.arange(STRATA), busiest].set(MOST).astype(jnp.int32)


def block_scale(rng, shape, shards, smallest, top_value):
    gain = 1.0
    for axis_at, blocks in shards:
        heights = jax.random.uniform(jax.random.fold_in(jax.random.fold_in(rng, 6), axis_at), (blocks,), jnp.float32, smallest / len(shards), top_value / len(shards))
        gain = gain * jnp.repeat(jnp.exp(heights), shape[axis_at] // blocks).reshape((-1,) + (1,) * (len(shape) - 1 - axis_at))
    return gain


def noise(rng, shape, deviation, most, split=(), dtype=jnp.bfloat16):
    array = deviation * jax.random.normal(rng, shape, jnp.float32)
    if split:
        array = array * block_scale(rng, shape, split, -0.22, 0.18)
    return jnp.clip(array, -most, most).astype(dtype)


def setup_inputs(seed: int = 0) -> dict:
    seeds = jax.random.split(jax.random.key(seed), 6)
    row_factors = draw_row_factors(jax.random.fold_in(seeds[5], 71), 0)
    col_factors = draw_col_factors(jax.random.fold_in(seeds[5], 71), 0)
    tile_values = noise(seeds[2], (STRATA, DEVICES * MOST, TILE, TILE), 1.0, 4.0, ((1, 32),))
    tile_coords = draw_tile_coords(jax.random.fold_in(seeds[5], 71), 0)
    tile_counts = draw_tile_counts(jax.random.fold_in(seeds[5], 71), 0)
    return {"row_factors": row_factors, "col_factors": col_factors, "tile_values": tile_values, "tile_coords": tile_coords, "tile_counts": tile_counts}


LEARN_RATE = 0.03
DECAY_RATE = 0.1


def through_half(value):
    return lax.optimization_barrier(value.astype(jnp.bfloat16)).astype(jnp.float32)


def picker(positions, extent, live_mask):
    return (positions[:, None] == jnp.arange(extent)[None, :]).astype(jnp.float32) * live_mask[:, None]


def update(packed):
    row_block, col_block, values, tile_pos, tile_count = packed
    high = lax.Precision.HIGHEST
    row_tiles = ROW_DEV // TILE
    col_tiles = COL_BLK // TILE
    live_mask = (jnp.arange(MOST) < tile_count).astype(jnp.float32)
    row_pick = picker(tile_pos[:, 0], row_tiles, live_mask)
    col_pick = picker(tile_pos[:, 1], col_tiles, live_mask)
    row_half = through_half(row_block).reshape(row_tiles, TILE, RANK)
    col_half = through_half(col_block).reshape(col_tiles, TILE, RANK)
    row_sel = jnp.einsum('tk,kia->tia', row_pick, row_half, precision=high)
    col_sel = jnp.einsum('tk,kja->tja', col_pick, col_half, precision=high)
    estimate = jnp.einsum('tia,tja->tij', row_sel, col_sel, precision=high)
    residue = through_half(values.astype(jnp.float32) - estimate)
    row_terms = jnp.einsum('tij,tja->tia', residue, col_sel, precision=high)
    col_terms = jnp.einsum('tij,tia->tja', residue, row_sel, precision=high)
    grad_rows = jnp.einsum('tk,tia->kia', row_pick, row_terms, precision=high).reshape(ROW_DEV, RANK)
    grad_cols = jnp.einsum('tk,tja->kja', col_pick, col_terms, precision=high).reshape(COL_BLK, RANK)
    new_rows = row_block + LEARN_RATE * (grad_rows - DECAY_RATE * row_block)
    new_cols = col_block + LEARN_RATE * (grad_cols - DECAY_RATE * col_block)
    return new_rows, new_cols


def reference(row_factors, col_factors, tile_values, tile_coords, tile_counts):
    row_blocks = row_factors.reshape(DEVICES, ROW_DEV, RANK)
    held = col_factors.reshape(DEVICES, COL_BLK, RANK)
    for stratum in range(STRATA):
        values = tile_values[stratum].reshape(DEVICES, MOST, TILE, TILE)
        tile_pos = tile_coords[stratum].reshape(DEVICES, MOST, 2)
        row_blocks, held = lax.map(update, (row_blocks, held, values, tile_pos, tile_counts[stratum]))
        if stratum + 1 < STRATA:
            grid = held.reshape(N_BLK, N_GROUP, COL_BLK, RANK)
            if stratum == 2:
                grid = jnp.roll(grid, 1, axis=1)
            else:
                grid = jnp.roll(grid, 1, axis=0)
            held = grid.reshape(DEVICES, COL_BLK, RANK)
    return row_blocks.reshape(ROWS, RANK), held.reshape(COLS, RANK)
```

```python
import functools

import jax
import jax.numpy as jnp
from jax import lax
from jax.experimental import pallas as pl
from jax.experimental.pallas import tpu as pltpu
from jax.sharding import PartitionSpec as P

STRATA = 5
LEARN_RATE = 0.03
DECAY_RATE = 0.1
CHUNKS = 2
SUBLANES = 8

VMEM = pl.BlockSpec(memory_space=pltpu.VMEM)
SMEM = pl.BlockSpec(memory_space=pltpu.SMEM)
ANY = pl.BlockSpec(memory_space=pl.ANY)


def params():
    return pltpu.CompilerParams(vmem_limit_bytes=24 * 1024 * 1024)


def cost(flops, moved):
    return pl.CostEstimate(flops=flops, bytes_accessed=moved, transcendentals=0)


def scatter(stratum, values, coords, counts, dense, live):
    listed, tile, _ = values.shape
    dense[...] = jnp.zeros_like(dense)
    live[...] = jnp.zeros_like(live)
    count = counts[stratum, 0]
    for t in range(listed):

        @pl.when(t < count)
        def _():
            r = coords[stratum, t, 0]
            c = pl.multiple_of(coords[stratum, t, 1] * tile, tile)
            dense[pl.ds(pl.multiple_of(r * tile, tile), tile), pl.ds(c, tile)] = values[t]
            named = lax.broadcasted_iota(jnp.int32, (SUBLANES, tile), 0) == r
            live[:, pl.ds(c, tile)] = jnp.where(named, 1.0, live[:, pl.ds(c, tile)])


def sgd(old, grad):
    return old + LEARN_RATE * (grad - DECAY_RATE * old)


def chunk_step(tile, rows, cols, dense, live):
    row_half = rows.astype(jnp.bfloat16)
    col_half = cols.astype(jnp.bfloat16)
    estimate = lax.dot_general(
        row_half, col_half, (((1,), (1,)), ((), ())), preferred_element_type=jnp.float32
    )
    parts = []
    for r in range(rows.shape[0] // tile):
        at = slice(r * tile, (r + 1) * tile)
        residue = dense[at].astype(jnp.float32) - estimate[at]
        parts.append(jnp.where(live[r : r + 1] > 0, residue, 0.0).astype(jnp.bfloat16))
    residue = jnp.concatenate(parts, axis=0)
    grad_rows = jnp.dot(residue, col_half, preferred_element_type=jnp.float32)
    grad_cols = lax.dot_general(
        residue, row_half, (((0,), (0,)), ((), ())), preferred_element_type=jnp.float32
    )
    return grad_rows, sgd(cols, grad_cols)


def first_kernel(u_ref, c_ref, x_ref, coords, counts, u_out, *rest):
    c_outs, (dense, live) = rest[:CHUNKS], rest[CHUNKS:]
    tile = x_ref.shape[2]
    scatter(0, x_ref.at[0], coords, counts, dense, live)
    rows = u_ref[...]
    width = c_ref.shape[0] // CHUNKS
    total = None
    for h in range(CHUNKS):
        at = slice(h * width, (h + 1) * width)
        grad, c_outs[h][...] = chunk_step(tile, rows, c_ref[at], dense[:, at], live[:, at])
        total = grad if total is None else total + grad
    u_out[...] = sgd(rows, total)


def first(u, c, values, coords, counts):
    rows, rank = u.shape
    cols = c.shape[0]
    _, listed, tile, _ = values.shape
    out = pl.pallas_call(
        first_kernel,
        grid=(1,),
        out_shape=[jax.ShapeDtypeStruct(u.shape, u.dtype)]
        + [jax.ShapeDtypeStruct((cols // CHUNKS, rank), c.dtype)] * CHUNKS,
        in_specs=[VMEM, VMEM, pl.BlockSpec((1, listed, tile, tile), lambda i: (0, 0, 0, 0)), SMEM, SMEM],
        out_specs=[VMEM] * (1 + CHUNKS),
        scratch_shapes=[
            pltpu.VMEM((rows, cols), jnp.bfloat16),
            pltpu.VMEM((SUBLANES, cols), jnp.float32),
        ],
        compiler_params=params(),
        cost_estimate=cost(6 * rows * cols * rank, 4 * rows * rank * 4),
        name="first_stratum",
    )(u, c, values, coords, counts)
    return out[0], out[1:]


def layout_kernel(x_ref, coords, counts, _, *outs):
    later = len(outs) // 2
    for s in range(later):
        scatter(s + 1, x_ref.at[s + 1], coords, counts, outs[s], outs[later + s])


def layout(values, coords, counts, rows, cols, after):
    strata = values.shape[0]
    out = pl.pallas_call(
        layout_kernel,
        out_shape=[jax.ShapeDtypeStruct((rows, cols), jnp.bfloat16)] * (strata - 1)
        + [jax.ShapeDtypeStruct((SUBLANES, cols), jnp.float32)] * (strata - 1),
        in_specs=[VMEM, SMEM, SMEM, ANY],
        out_specs=[VMEM] * (2 * (strata - 1)),
        compiler_params=params(),
        cost_estimate=cost(0, 8 * rows * cols),
        name="lay_out_tiles",
    )(values, coords, counts, after)
    return list(zip(out[: strata - 1], out[strata - 1 :]))


def chunk_kernel(h, parity, tile, u_ref, c_ref, dense, live, *rest):
    last = h == CHUNKS - 1
    acc_ref = rest[0] if h else None
    u_out, c_out = rest[-2:]
    width = c_ref.shape[0]

    def body():
        at = slice(h * width, (h + 1) * width)
        rows = u_ref[...]
        grad, c_out[...] = chunk_step(tile, rows, c_ref[...], dense[:, at], live[:, at])
        if h:
            grad = grad + acc_ref[...]
        u_out[...] = sgd(rows, grad) if last else grad

    if parity is None:
        body()
        return
    mine = lax.axis_index("blk") % 2 == parity
    pl.when(mine)(body)
    if last:

        @pl.when(jnp.logical_not(mine))
        def _():
            u_out[...] = u_ref[...]


def chunk(h, parity, tile, u, c, laid, acc):
    dense, live = laid
    operands = [u, c, dense, live] + ([acc] if h else [])
    return pl.pallas_call(
        functools.partial(chunk_kernel, h, parity, tile),
        out_shape=[jax.ShapeDtypeStruct(u.shape, u.dtype), jax.ShapeDtypeStruct(c.shape, c.dtype)],
        in_specs=[VMEM] * len(operands),
        out_specs=[VMEM] * 2,
        compiler_params=params(),
        cost_estimate=cost(6 * u.size * c.shape[0], 4 * u.size * 4),
        name="chunk_step",
    )(*operands)


def stratum_chunks(parity, tile, u, cs, laid):
    acc, outs = None, []
    for h in range(CHUNKS):
        acc, c = chunk(h, parity, tile, u, cs[h], laid, acc)
        outs.append(c)
    return acc, outs


def send(chunks, axis, senders):
    n = lax.axis_size(axis)
    return [lax.ppermute(c, axis, [(i, (i + 1) % n) for i in senders]) for c in chunks]


def send_group(chunks, parity):
    blk, group = lax.axis_size("blk"), lax.axis_size("group")
    route = [
        (b * group + g, b * group + (g + 1) % group)
        for b in range(parity, blk, 2)
        for g in range(group)
    ]
    return [lax.ppermute(c, ("blk", "group"), route) for c in chunks]


def per_device(row_factors, col_factors, tile_values, tile_coords, tile_counts):
    u, c = row_factors, col_factors
    tile = tile_values.shape[2]
    blk = lax.axis_size("blk")
    even, odd = range(0, blk, 2), range(1, blk, 2)

    u, c0 = first(u, c, tile_values, tile_coords, tile_counts)
    to_even = send(c0, "blk", odd)
    to_odd = send(c0, "blk", even)
    laid = layout(tile_values, tile_coords, tile_counts, u.shape[0], c.shape[0], c0[-1])
    u, odd1 = stratum_chunks(1, tile, u, to_odd, laid[0])
    u, even1 = stratum_chunks(0, tile, u, to_even, laid[0])
    to_even = send(odd1, "blk", odd)
    to_odd = send(even1, "blk", even)
    u, odd2 = stratum_chunks(1, tile, u, to_odd, laid[1])
    u, even2 = stratum_chunks(0, tile, u, to_even, laid[1])
    odd3 = send_group(odd2, 1)
    even3 = send_group(even2, 0)
    u, odd3 = stratum_chunks(1, tile, u, odd3, laid[2])
    u, even3 = stratum_chunks(0, tile, u, even3, laid[2])
    to_even = send(odd3, "blk", odd)
    to_odd = send(even3, "blk", even)
    cs = [a + b for a, b in zip(to_even, to_odd)]
    u, cs = stratum_chunks(None, tile, u, cs, laid[3])
    return u, jnp.concatenate(cs, axis=0)


def solution(mesh):
    return jax.shard_map(
        per_device,
        mesh=mesh,
        in_specs=(
            P(("blk", "group"), None),
            P(("blk", "group"), None),
            P(None, ("blk", "group"), None, None),
            P(None, ("blk", "group"), None),
            P(None, ("blk", "group")),
        ),
        out_specs=(P(("blk", "group"), None), P(("blk", "group"), None)),
        check_vma=False,
    )
```

```python
import functools

import jax
import jax.numpy as jnp
from jax import lax
from jax.experimental import pallas as pl
from jax.experimental.pallas import tpu as pltpu
from jax.sharding import PartitionSpec as P

LEARN_RATE = 0.03
DECAY_RATE = 0.1
CHUNKS = 4
SUBLANES = 8

VMEM = pl.BlockSpec(memory_space=pltpu.VMEM)
SMEM = pl.BlockSpec(memory_space=pltpu.SMEM)
HBM = pl.BlockSpec(memory_space=pltpu.HBM)
ANY = pl.BlockSpec(memory_space=pl.ANY)


def call(body, name, operands, in_specs, outs, out_specs, flops=0, moved=0, aliases=None, scratch=(), vmem=24):
    return pl.pallas_call(
        body,
        out_shape=outs,
        in_specs=in_specs,
        out_specs=out_specs,
        input_output_aliases=aliases or {},
        scratch_shapes=list(scratch),
        compiler_params=pltpu.CompilerParams(vmem_limit_bytes=vmem * 1024 * 1024),
        cost_estimate=pl.CostEstimate(flops=flops, bytes_accessed=moved, transcendentals=0),
        name=name,
    )(*operands)


def like(array, shape=None, dtype=None):
    return jax.ShapeDtypeStruct(shape or array.shape, dtype or array.dtype)


def scatter(stratum, values, coords, counts, dense, live):
    listed, tile, _ = values.shape
    dense[...] = jnp.zeros_like(dense)
    live[...] = jnp.zeros_like(live)
    for t in range(listed):

        @pl.when(t < counts[0, stratum])
        def _():
            r = coords[stratum, 0, t]
            c = pl.multiple_of(coords[stratum, 1, t] * tile, tile)
            dense[pl.ds(pl.multiple_of(r * tile, tile), tile), pl.ds(c, tile)] = values[t]
            named = lax.broadcasted_iota(jnp.int32, (SUBLANES, tile), 0) == r
            live[:, pl.ds(c, tile)] = jnp.where(named, 1.0, live[:, pl.ds(c, tile)])


def sgd(old, grad):
    return old + LEARN_RATE * (grad - DECAY_RATE * old)


def chunk_step(tile, rows, cols, dense, live):
    row_half = rows.astype(jnp.bfloat16)
    col_half = cols.astype(jnp.bfloat16)
    estimate = lax.dot_general(
        row_half, col_half, (((1,), (1,)), ((), ())), preferred_element_type=jnp.float32
    )
    parts = []
    for r in range(rows.shape[0] // tile):
        at = slice(r * tile, (r + 1) * tile)
        residue = dense[at].astype(jnp.float32) - estimate[at]
        parts.append(jnp.where(live[r : r + 1] > 0, residue, 0.0).astype(jnp.bfloat16))
    residue = jnp.concatenate(parts, axis=0)
    grad_cols = lax.dot_general(
        residue, row_half, (((0,), (0,)), ((), ())), preferred_element_type=jnp.float32
    )
    grad_rows = jnp.dot(residue, col_half, preferred_element_type=jnp.float32)
    return grad_rows, sgd(cols, grad_cols)


def span(h, width):
    return slice(h * width, (h + 1) * width)


def first_kernel(u_hbm, c_hbm, x_hbm, coords_hbm, counts_hbm, *refs):
    u_ref, acc, dense, live, c_out = refs[:5]
    c_rest = refs[5 : 4 + CHUNKS]
    x_ref, c_ref, coords, counts, sems = refs[4 + CHUNKS :]
    width, tile = c_ref.shape[0], x_ref.shape[1]
    pairs = [(coords_hbm, coords), (counts_hbm, counts), (x_hbm.at[0], x_ref), (u_hbm, u_ref)]
    pairs += [(c_hbm.at[pl.ds(0, width)], c_ref)]
    pairs += [(c_hbm.at[pl.ds((i + 1) * width, width)], c) for i, c in enumerate(c_rest)]
    copies = [pltpu.make_async_copy(s, d, sems.at[i]) for i, (s, d) in enumerate(pairs)]
    for copy in copies:
        copy.start()
    for copy in copies[:3]:
        copy.wait()
    scatter(0, x_ref, coords, counts, dense, live)
    for copy in copies[3:5]:
        copy.wait()
    at = span(0, width)
    acc[...], c_out[...] = chunk_step(tile, u_ref[...], c_ref[...], dense[:, at], live[:, at])
    for copy in copies[5:]:
        copy.wait()


def first(u, c, values, coords, counts):
    rows, cols = u.shape[0], c.shape[0]
    part = (cols // CHUNKS, c.shape[1])
    outs = [like(u), like(u), like(u, (rows, cols), jnp.bfloat16), like(u, (SUBLANES, cols))]
    outs += [like(c, part)] * CHUNKS
    operands = [pltpu.with_memory_space_constraint(x, pltpu.HBM) for x in (u, c, values, coords, counts)]
    u, acc, dense, live, done, *rest = call(
        first_kernel,
        "first_chunk",
        operands,
        [HBM] * 5,
        outs,
        [VMEM] * len(outs),
        flops=6 * u.size * part[0],
        moved=8 * u.size,
        scratch=[
            pltpu.VMEM(values.shape[1:], values.dtype),
            pltpu.VMEM(part, c.dtype),
            pltpu.SMEM(coords.shape, coords.dtype),
            pltpu.SMEM(counts.shape, counts.dtype),
            pltpu.SemaphoreType.DMA((4 + CHUNKS,)),
        ],
    )
    return u, acc, (dense, live), done, rest


def layout_kernel(x_ref, coords, counts, _, *outs):
    later = len(outs) // 2
    for s in range(later):
        scatter(s + 1, x_ref.at[s + 1], coords, counts, outs[s], outs[later + s])


def layout(values, coords, counts, rows, cols, after):
    later = values.shape[0] - 1
    outs = [like(values, (rows, cols))] * later
    outs += [like(values, (SUBLANES, cols), jnp.float32)] * later
    out = call(
        layout_kernel,
        "lay_out_tiles",
        (values, coords, counts, after),
        [VMEM, SMEM, SMEM, ANY],
        outs,
        [VMEM] * len(outs),
        moved=8 * rows * cols,
    )
    return list(zip(out[:later], out[later:]))


def chunk_kernel(h, tile, u_ref, c_ref, dense, live, *rest):
    u_out, c_out = rest[-2:]
    last = h == CHUNKS - 1
    at = span(h, c_ref.shape[0])
    rows = u_out[...] if last else u_ref[...]
    grad, c_out[...] = chunk_step(tile, rows, c_ref[...], dense[:, at], live[:, at])
    if h:
        grad = grad + rest[0][...]
    u_out[...] = sgd(rows, grad) if last else grad


def chunk(h, tile, u, c, laid, acc):
    operands = [u, c, *laid] + ([acc] if h else [])
    return call(
        functools.partial(chunk_kernel, h, tile),
        "chunk_step",
        operands,
        [VMEM] * len(operands),
        [like(u), like(c)],
        [VMEM] * 2,
        flops=6 * u.size * c.shape[0],
        moved=16 * u.size,
        aliases={0: 0} if h == CHUNKS - 1 else None,
    )


def final_kernel(h, tile, u_ref, c_in, dense, live, *rest):
    width = c_in.shape[0]
    at, place = span(h, width), pl.ds(h * width, width)
    last = h == CHUNKS - 1
    acc_in, rest = (rest[0], rest[2:]) if h else (None, rest)
    first_out, c_hbm, *scratch = rest
    c_new, sems = scratch[-2:]
    rows = u_ref[...]
    grad, c_new[...] = chunk_step(tile, rows, c_in[...], dense[:, at], live[:, at])
    copies = [pltpu.make_async_copy(c_new, c_hbm.at[place], sems.at[0])]
    copies[0].start()
    for r in range(rows.shape[0] // tile):
        part = span(r, tile)
        total = grad[part] if acc_in is None else grad[part] + acc_in[part]
        if last:
            u_new = scratch[0]
            u_new[part] = sgd(rows[part], total)
            rows_at = pl.ds(r * tile, tile)
            copies.append(pltpu.make_async_copy(u_new.at[rows_at], first_out.at[rows_at], sems.at[r + 1]))
            copies[-1].start()
        else:
            first_out[part] = total
    for copy in copies:
        copy.wait()


def final(tile, u, cs, laid):
    part = cs[0]
    whole = like(part, (part.shape[0] * CHUNKS, part.shape[1]))
    carried = []
    for h in range(CHUNKS):
        last = h == CHUNKS - 1
        operands = (u, cs[h], *laid, *carried)
        carried = call(
            functools.partial(final_kernel, h, tile),
            "final_chunk",
            operands,
            [VMEM] * 4 + ([VMEM, HBM] if h else []),
            [like(u), whole],
            [HBM if last else VMEM, HBM],
            flops=6 * u.size * part.shape[0],
            moved=16 * u.size,
            aliases={5: 1} if h else None,
            scratch=([pltpu.VMEM(u.shape, u.dtype)] if last else [])
            + [
                pltpu.VMEM(part.shape, part.dtype),
                pltpu.SemaphoreType.DMA((1 + u.shape[0] // tile,)),
            ],
        )
    return carried


def shifted(chunk, axis):
    n = lax.axis_size(axis)
    return lax.ppermute(chunk, axis, [(i, (i + 1) % n) for i in range(n)])


def per_device(row_factors, col_factors, tile_values, tile_coords, tile_counts):
    tile = tile_values.shape[2]
    strata = tile_values.shape[0]
    coords, counts = tile_coords.transpose(0, 2, 1), tile_counts.transpose(1, 0)
    u, acc, laid0, done, rest = first(row_factors, col_factors, tile_values, coords, counts)
    cs = [shifted(done, "blk")]
    for h in range(1, CHUNKS):
        acc, done = chunk(h, tile, u, rest[h - 1], laid0, acc)
        cs.append(shifted(done, "blk"))
    u = acc
    laid = layout(tile_values, coords, counts, u.shape[0], col_factors.shape[0], done)
    for stratum in range(1, strata - 1):
        axis = "group" if stratum == 2 else "blk"
        acc, arrived, cs = None, cs, []
        for h in range(CHUNKS):
            acc, done = chunk(h, tile, u, arrived[h], laid[stratum - 1], acc)
            cs.append(shifted(done, axis))
        u = acc
    return final(tile, u, cs, laid[-1])


def solution(mesh):
    return jax.shard_map(
        per_device,
        mesh=mesh,
        in_specs=(
            P(("blk", "group"), None),
            P(("blk", "group"), None),
            P(None, ("blk", "group"), None, None),
            P(None, ("blk", "group"), None),
            P(None, ("blk", "group")),
        ),
        out_specs=(P(("blk", "group"), None), P(("blk", "group"), None)),
        check_vma=False,
    )
```

```python
import functools

import jax
import jax.numpy as jnp
from jax import lax
from jax.experimental import pallas as pl
from jax.experimental.pallas import tpu as pltpu
from jax.sharding import PartitionSpec as P

LEARN_RATE = 0.03
DECAY_RATE = 0.1
CHUNKS = 4
SUBLANES = 8

VMEM = pl.BlockSpec(memory_space=pltpu.VMEM)
SMEM = pl.BlockSpec(memory_space=pltpu.SMEM)
HBM = pl.BlockSpec(memory_space=pltpu.HBM)
ANY = pl.BlockSpec(memory_space=pl.ANY)


def call(body, name, operands, in_specs, outs, out_specs, flops=0, moved=0, aliases=None, scratch=()):
    return pl.pallas_call(
        body,
        out_shape=outs,
        in_specs=in_specs,
        out_specs=out_specs,
        input_output_aliases=aliases or {},
        scratch_shapes=list(scratch),
        compiler_params=pltpu.CompilerParams(vmem_limit_bytes=24 * 1024 * 1024),
        cost_estimate=pl.CostEstimate(flops=flops, bytes_accessed=moved, transcendentals=0),
        name=name,
    )(*operands)


def like(array, shape=None, dtype=None):
    return jax.ShapeDtypeStruct(shape or array.shape, dtype or array.dtype)


def span(h, width):
    return slice(h * width, (h + 1) * width)


def scatter(stratum, values, coords, counts, dense, live):
    listed, tile, _ = values.shape
    dense[...] = jnp.zeros_like(dense)
    live[...] = jnp.zeros_like(live)
    for t in range(listed):

        @pl.when(t < counts[0, stratum])
        def _():
            r = pl.multiple_of(coords[stratum, 0, t] * tile, tile)
            c = coords[stratum, 1, t]
            dense[pl.ds(pl.multiple_of(c * tile, tile), tile), pl.ds(r, tile)] = values[t].T
            named = lax.broadcasted_iota(jnp.int32, (SUBLANES, tile), 0) == c
            live[:, pl.ds(r, tile)] = jnp.where(named, 1.0, live[:, pl.ds(r, tile)])


def sgd(old, grad):
    return old + LEARN_RATE * (grad - DECAY_RATE * old)


def dot(a, b, contract):
    return lax.dot_general(a, b, (contract, ((), ())), preferred_element_type=jnp.float32)


def columns_step(first_tile, tile, row_half, cols, dense, live):
    estimate = dot(cols.astype(jnp.bfloat16), row_half, ((1,), (1,)))
    parts = []
    for i in range(cols.shape[0] // tile):
        at = span(i, tile)
        residue = dense[at].astype(jnp.float32) - estimate[at]
        named = live[first_tile + i : first_tile + i + 1] > 0
        parts.append(jnp.where(named, residue, 0.0).astype(jnp.bfloat16))
    residue = parts[0] if len(parts) == 1 else jnp.concatenate(parts, axis=0)
    return residue, sgd(cols, dot(residue, row_half, ((1,), (0,))))


def rows_gradient(residues, cols):
    return sum(
        dot(e[...], c[...].astype(jnp.bfloat16), ((0,), (0,))) for e, c in zip(residues, cols)
    )


def first_kernel(u_hbm, c_hbm, x_hbm, coords_hbm, counts_hbm, *refs):
    u_ref, c_ref, residue = refs[:3]
    c_outs = refs[3 : 3 + CHUNKS]
    dense, live, x_ref, coords, counts, sems = refs[3 + CHUNKS :]
    tile = x_ref.shape[1]
    pairs = [(coords_hbm, coords), (counts_hbm, counts), (x_hbm.at[0], x_ref)]
    pairs += [(u_hbm, u_ref), (c_hbm, c_ref)]
    copies = [pltpu.make_async_copy(s, d, sems.at[i]) for i, (s, d) in enumerate(pairs)]
    for copy in copies:
        copy.start()
    for copy in copies[:3]:
        copy.wait()
    scatter(0, x_ref, coords, counts, dense, live)
    for copy in copies[3:]:
        copy.wait()
    row_half = u_ref[...].astype(jnp.bfloat16)
    for h in range(CHUNKS):
        at = span(h, c_ref.shape[0] // CHUNKS)
        first_tile = at.start // tile
        residue[at], c_outs[h][...] = columns_step(
            first_tile, tile, row_half, c_ref[at], dense[at], live
        )


def first(u, c, values, coords, counts):
    rows, cols = u.shape[0], c.shape[0]
    part = (cols // CHUNKS, c.shape[1])
    outs = [like(u), like(c), like(u, (cols, rows), jnp.bfloat16)] + [like(c, part)] * CHUNKS
    operands = (u, c, values, coords, counts)
    u, c, residue, *cs = call(
        first_kernel,
        "first_columns",
        [pltpu.with_memory_space_constraint(x, pltpu.HBM) for x in operands],
        [HBM] * 5,
        outs,
        [VMEM] * len(outs),
        flops=4 * u.size * cols,
        moved=8 * u.size,
        scratch=[
            pltpu.VMEM((cols, rows), jnp.bfloat16),
            pltpu.VMEM((SUBLANES, rows), jnp.float32),
            pltpu.VMEM(values.shape[1:], values.dtype),
            pltpu.SMEM(coords.shape, coords.dtype),
            pltpu.SMEM(counts.shape, counts.dtype),
            pltpu.SemaphoreType.DMA((5,)),
        ],
    )
    return u, c, residue, cs


def layout_kernel(stratum, x_ref, coords, counts, _, dense, live):
    scatter(stratum, x_ref.at[stratum], coords, counts, dense, live)


def layout(stratum, values, coords, counts, rows, cols, after):
    return call(
        functools.partial(layout_kernel, stratum),
        "lay_out_tiles",
        (values, coords, counts, after),
        [VMEM, SMEM, SMEM, ANY],
        [like(values, (cols, rows)), like(values, (SUBLANES, rows), jnp.float32)],
        [VMEM] * 2,
        moved=4 * rows * cols,
    )


def columns_kernel(h, tile, row_half, c_ref, dense, live, c_out, residue):
    width = c_ref.shape[0]
    residue[...], c_out[...] = columns_step(
        h * width // tile, tile, row_half[...], c_ref[...], dense[span(h, width)], live
    )


def columns(h, tile, row_half, c, laid):
    return call(
        functools.partial(columns_kernel, h, tile),
        "columns_step",
        (row_half, c, *laid),
        [VMEM] * 4,
        [like(c), like(row_half, (c.shape[0], row_half.shape[0]))],
        [VMEM] * 2,
        flops=4 * row_half.size * c.shape[0],
        moved=2 * row_half.size + 8 * c.size,
    )


def rows_kernel(*refs):
    *refs, u_out, half_out = refs
    u_ref, pairs = refs[0], refs[1:]
    n = len(pairs) // 2
    u_new = sgd(u_ref[...], rows_gradient(pairs[:n], pairs[n:]))
    u_out[...] = u_new
    half_out[...] = u_new.astype(jnp.bfloat16)


def rows(u, residues, cols):
    operands = (u, *residues, *cols)
    return call(
        rows_kernel,
        "rows_step",
        operands,
        [VMEM] * len(operands),
        [like(u), like(u, dtype=jnp.bfloat16)],
        [VMEM] * 2,
        flops=2 * u.size * sum(c.shape[0] for c in cols),
        moved=10 * u.size,
    )


def before_last_kernel(*refs):
    n = CHUNKS - 1
    residues, cols, done = refs[:n], refs[n : 2 * n], refs[2 * n : 3 * n]
    acc, c_hbm, sems = refs[3 * n :]
    width = done[0].shape[0]
    copies = [
        pltpu.make_async_copy(c, c_hbm.at[pl.ds(h * width, width)], sems.at[h])
        for h, c in enumerate(done)
    ]
    for copy in copies:
        copy.start()
    acc[...] = rows_gradient(residues, cols)
    for copy in copies:
        copy.wait()


def last_kernel(tile, u_ref, row_half, c_ref, dense, live, acc, _, u_hbm, c_hbm, u_new, c_new, sems):
    h, width = CHUNKS - 1, c_ref.shape[0]
    cols = c_ref[...]
    residue, c_new[...] = columns_step(
        h * width // tile, tile, row_half[...], cols, dense[span(h, width)], live
    )
    copies = [pltpu.make_async_copy(c_new, c_hbm.at[pl.ds(h * width, width)], sems.at[0])]
    copies[0].start()
    col_half = cols.astype(jnp.bfloat16)
    for r in range(u_ref.shape[0] // tile):
        part, place = span(r, tile), pl.ds(r * tile, tile)
        grad = dot(residue[:, part], col_half, ((0,), (0,)))
        u_new[part] = sgd(u_ref[part], acc[part] + grad)
        copies.append(pltpu.make_async_copy(u_new.at[place], u_hbm.at[place], sems.at[r + 1]))
        copies[-1].start()
    for copy in copies:
        copy.wait()


def final(tile, u, row_half, cs, laid):
    n = CHUNKS - 1
    width, rank = cs[0].shape
    whole = like(cs[0], (CHUNKS * width, rank))
    done, residues = [], []
    for h in range(n):
        c, residue = columns(h, tile, row_half, cs[h], laid)
        done.append(c)
        residues.append(residue)
    acc, out = call(
        before_last_kernel,
        "rows_before_last",
        (*residues, *cs[:n], *done),
        [VMEM] * (3 * n),
        [like(u), whole],
        [VMEM, HBM],
        flops=2 * u.size * n * width,
        moved=8 * u.size,
        scratch=[pltpu.SemaphoreType.DMA((n,))],
    )
    return call(
        functools.partial(last_kernel, tile),
        "last_columns_and_rows",
        (u, row_half, cs[n], *laid, acc, out),
        [VMEM] * 6 + [HBM],
        [like(u), whole],
        [HBM, HBM],
        flops=6 * u.size * width,
        moved=8 * u.size,
        aliases={6: 1},
        scratch=[
            pltpu.VMEM(u.shape, u.dtype),
            pltpu.VMEM((width, rank), u.dtype),
            pltpu.SemaphoreType.DMA((1 + u.shape[0] // tile,)),
        ],
    )


def shifted(chunk, axis):
    n = lax.axis_size(axis)
    return lax.ppermute(chunk, axis, [(i, (i + 1) % n) for i in range(n)])


def per_device(row_factors, col_factors, tile_values, tile_coords, tile_counts):
    tile = tile_values.shape[2]
    strata = tile_values.shape[0]
    coords, counts = tile_coords.transpose(0, 2, 1), tile_counts.transpose(1, 0)
    sizes = row_factors.shape[0], col_factors.shape[0]
    u, c, residue, done = first(row_factors, col_factors, tile_values, coords, counts)
    cs = [shifted(d, "blk") for d in done]
    u, row_half = rows(u, [residue], [c])
    for stratum in range(1, strata):
        laid = layout(stratum, tile_values, coords, counts, *sizes, done[-1])
        if stratum == strata - 1:
            return final(tile, u, row_half, cs, laid)
        axis = "group" if stratum == 2 else "blk"
        arrived, cs, done, residues = cs, [], [], []
        for h in range(CHUNKS):
            d, residue = columns(h, tile, row_half, arrived[h], laid)
            done.append(d)
            residues.append(residue)
            cs.append(shifted(d, axis))
        u, row_half = rows(u, residues, arrived)


def solution(mesh):
    return jax.shard_map(
        per_device,
        mesh=mesh,
        in_specs=(
            P(("blk", "group"), None),
            P(("blk", "group"), None),
            P(None, ("blk", "group"), None, None),
            P(None, ("blk", "group"), None),
            P(None, ("blk", "group")),
        ),
        out_specs=(P(("blk", "group"), None), P(("blk", "group"), None)),
        check_vma=False,
    )
```

```python
import functools

import jax
import jax.numpy as jnp
from jax import lax
from jax.experimental import pallas as pl
from jax.experimental.pallas import tpu as pltpu
from jax.sharding import PartitionSpec as P

LEARN_RATE = 0.03
DECAY_RATE = 0.1
CHUNKS = 4
SUBLANES = 8

VMEM = pl.BlockSpec(memory_space=pltpu.VMEM)
SMEM = pl.BlockSpec(memory_space=pltpu.SMEM)
HBM = pl.BlockSpec(memory_space=pltpu.HBM)
ANY = pl.BlockSpec(memory_space=pl.ANY)


def call(body, name, operands, in_specs, outs, out_specs, flops=0, moved=0, aliases=None, scratch=()):
    return pl.pallas_call(
        body,
        out_shape=outs,
        in_specs=in_specs,
        out_specs=out_specs,
        input_output_aliases=aliases or {},
        scratch_shapes=list(scratch),
        compiler_params=pltpu.CompilerParams(vmem_limit_bytes=24 * 1024 * 1024),
        cost_estimate=pl.CostEstimate(flops=flops, bytes_accessed=moved, transcendentals=0),
        name=name,
    )(*operands)


def like(array, shape=None, dtype=None):
    return jax.ShapeDtypeStruct(shape or array.shape, dtype or array.dtype)


def span(h, width):
    return slice(h * width, (h + 1) * width)


def scatter(stratum, values, coords, counts, dense, live):
    listed, tile, _ = values.shape
    col = lax.broadcasted_iota(jnp.int32, live.shape, 0)
    row = lax.broadcasted_iota(jnp.int32, live.shape, 1)
    named = jnp.zeros(live.shape, jnp.float32)
    for t in range(listed):
        r = pl.multiple_of(coords[stratum, 0, t] * tile, tile)
        c = coords[stratum, 1, t]
        dense[pl.ds(pl.multiple_of(c * tile, tile), tile), pl.ds(r, tile)] = values[t].T
        alive_c = jnp.where(t < counts[0, stratum], c, -1)
        named = jnp.where((col == alive_c) & (row >= r) & (row < r + tile), 1.0, named)
    live[...] = named


def sgd(old, grad):
    return old + LEARN_RATE * (grad - DECAY_RATE * old)


def dot(a, b, contract):
    return lax.dot_general(a, b, (contract, ((), ())), preferred_element_type=jnp.float32)


def columns_step(first_tile, tile, row_half, cols, dense, live):
    estimate = dot(cols.astype(jnp.bfloat16), row_half, ((1,), (1,)))
    parts = []
    for i in range(cols.shape[0] // tile):
        at = span(i, tile)
        residue = dense[at].astype(jnp.float32) - estimate[at]
        named = live[first_tile + i : first_tile + i + 1] > 0
        parts.append(jnp.where(named, residue, 0.0).astype(jnp.bfloat16))
    residue = parts[0] if len(parts) == 1 else jnp.concatenate(parts, axis=0)
    return residue, sgd(cols, dot(residue, row_half, ((1,), (0,))))


def rows_gradient(residues, cols):
    return sum(
        dot(e[...], c[...].astype(jnp.bfloat16), ((0,), (0,))) for e, c in zip(residues, cols)
    )


def first_kernel(u_hbm, c_hbm, x_hbm, coords_hbm, counts_hbm, *refs):
    u_ref, c_ref, residue = refs[:3]
    c_outs = refs[3 : 3 + CHUNKS]
    dense, live, x_ref, coords, counts, sems = refs[3 + CHUNKS :]
    tile = x_ref.shape[1]
    pairs = [(coords_hbm, coords), (counts_hbm, counts), (x_hbm.at[0], x_ref)]
    pairs += [(u_hbm, u_ref), (c_hbm, c_ref)]
    copies = [pltpu.make_async_copy(s, d, sems.at[i]) for i, (s, d) in enumerate(pairs)]
    for copy in copies:
        copy.start()
    for copy in copies[:3]:
        copy.wait()
    scatter(0, x_ref, coords, counts, dense, live)
    for copy in copies[3:]:
        copy.wait()
    row_half = u_ref[...].astype(jnp.bfloat16)
    for h in range(CHUNKS):
        at = span(h, c_ref.shape[0] // CHUNKS)
        first_tile = at.start // tile
        residue[at], c_outs[h][...] = columns_step(
            first_tile, tile, row_half, c_ref[at], dense[at], live
        )


def first(u, c, values, coords, counts):
    rows, cols = u.shape[0], c.shape[0]
    part = (cols // CHUNKS, c.shape[1])
    outs = [like(u), like(c), like(u, (cols, rows), jnp.bfloat16)] + [like(c, part)] * CHUNKS
    operands = (u, c, values, coords, counts)
    u, c, residue, *cs = call(
        first_kernel,
        "first_columns",
        [pltpu.with_memory_space_constraint(x, pltpu.HBM) for x in operands],
        [HBM] * 5,
        outs,
        [VMEM] * len(outs),
        flops=4 * u.size * cols,
        moved=8 * u.size,
        scratch=[
            pltpu.VMEM((cols, rows), jnp.bfloat16),
            pltpu.VMEM((SUBLANES, rows), jnp.float32),
            pltpu.VMEM(values.shape[1:], values.dtype),
            pltpu.SMEM(coords.shape, coords.dtype),
            pltpu.SMEM(counts.shape, counts.dtype),
            pltpu.SemaphoreType.DMA((5,)),
        ],
    )
    return u, c, residue, cs


def layout_kernel(stratum, x_ref, coords, counts, _, dense, live):
    scatter(stratum, x_ref.at[stratum], coords, counts, dense, live)


def layout(stratum, values, coords, counts, rows, cols, after):
    return call(
        functools.partial(layout_kernel, stratum),
        "lay_out_tiles",
        (values, coords, counts, after),
        [VMEM, SMEM, SMEM, ANY],
        [like(values, (cols, rows)), like(values, (SUBLANES, rows), jnp.float32)],
        [VMEM] * 2,
        moved=4 * rows * cols,
    )


def columns_kernel(h, tile, row_half, c_ref, dense, live, c_out, residue):
    width = c_ref.shape[0]
    residue[...], c_out[...] = columns_step(
        h * width // tile, tile, row_half[...], c_ref[...], dense[span(h, width)], live
    )


def columns(h, tile, row_half, c, laid):
    return call(
        functools.partial(columns_kernel, h, tile),
        "columns_step",
        (row_half, c, *laid),
        [VMEM] * 4,
        [like(c), like(row_half, (c.shape[0], row_half.shape[0]))],
        [VMEM] * 2,
        flops=4 * row_half.size * c.shape[0],
        moved=2 * row_half.size + 8 * c.size,
    )


def rows_kernel(*refs):
    *refs, u_out, half_out = refs
    u_ref, pairs = refs[0], refs[1:]
    n = len(pairs) // 2
    u_new = sgd(u_ref[...], rows_gradient(pairs[:n], pairs[n:]))
    u_out[...] = u_new
    half_out[...] = u_new.astype(jnp.bfloat16)


def rows(u, residues, cols):
    operands = (u, *residues, *cols)
    return call(
        rows_kernel,
        "rows_step",
        operands,
        [VMEM] * len(operands),
        [like(u), like(u, dtype=jnp.bfloat16)],
        [VMEM] * 2,
        flops=2 * u.size * sum(c.shape[0] for c in cols),
        moved=10 * u.size,
    )


def before_last_kernel(*refs):
    n = CHUNKS - 1
    residues, cols, done = refs[:n], refs[n : 2 * n], refs[2 * n : 3 * n]
    acc, c_hbm, sems = refs[3 * n :]
    width = done[0].shape[0]
    copies = [
        pltpu.make_async_copy(c, c_hbm.at[pl.ds(h * width, width)], sems.at[h])
        for h, c in enumerate(done)
    ]
    for copy in copies:
        copy.start()
    acc[...] = rows_gradient(residues, cols)
    for copy in copies:
        copy.wait()


def last_kernel(tile, u_ref, row_half, c_ref, dense, live, acc, _, u_hbm, c_hbm, u_new, c_new, sems):
    h, width = CHUNKS - 1, c_ref.shape[0]
    cols = c_ref[...]
    residue, new_cols = columns_step(
        h * width // tile, tile, row_half[...], cols, dense[span(h, width)], live
    )
    copies = []
    col_half = cols.astype(jnp.bfloat16)
    for r in range(u_ref.shape[0] // tile):
        part, place = span(r, tile), pl.ds(r * tile, tile)
        grad = dot(residue[:, part], col_half, ((0,), (0,)))
        u_new[part] = sgd(u_ref[part], acc[part] + grad)
        copies.append(pltpu.make_async_copy(u_new.at[place], u_hbm.at[place], sems.at[r]))
        copies[-1].start()
    c_new[...] = new_cols
    copies.append(pltpu.make_async_copy(c_new, c_hbm.at[pl.ds(h * width, width)], sems.at[len(copies)]))
    copies[-1].start()
    for copy in copies:
        copy.wait()


def final(tile, u, row_half, cs, laid):
    n = CHUNKS - 1
    width, rank = cs[0].shape
    whole = like(cs[0], (CHUNKS * width, rank))
    done, residues = [], []
    for h in range(n):
        c, residue = columns(h, tile, row_half, cs[h], laid)
        done.append(c)
        residues.append(residue)
    acc, out = call(
        before_last_kernel,
        "rows_before_last",
        (*residues, *cs[:n], *done),
        [VMEM] * (3 * n),
        [like(u), whole],
        [VMEM, HBM],
        flops=2 * u.size * n * width,
        moved=8 * u.size,
        scratch=[pltpu.SemaphoreType.DMA((n,))],
    )
    return call(
        functools.partial(last_kernel, tile),
        "last_columns_and_rows",
        (u, row_half, cs[n], *laid, acc, out),
        [VMEM] * 6 + [HBM],
        [like(u), whole],
        [HBM, HBM],
        flops=6 * u.size * width,
        moved=8 * u.size,
        aliases={6: 1},
        scratch=[
            pltpu.VMEM(u.shape, u.dtype),
            pltpu.VMEM((width, rank), u.dtype),
            pltpu.SemaphoreType.DMA((1 + u.shape[0] // tile,)),
        ],
    )


def shifted(chunk, axis):
    n = lax.axis_size(axis)
    return lax.ppermute(chunk, axis, [(i, (i + 1) % n) for i in range(n)])


def per_device(row_factors, col_factors, tile_values, tile_coords, tile_counts):
    tile = tile_values.shape[2]
    strata = tile_values.shape[0]
    coords, counts = tile_coords.transpose(0, 2, 1), tile_counts.transpose(1, 0)
    sizes = row_factors.shape[0], col_factors.shape[0]
    u, c, residue, done = first(row_factors, col_factors, tile_values, coords, counts)
    cs = [shifted(d, "blk") for d in done]
    u, row_half = rows(u, [residue], [c])
    for stratum in range(1, strata):
        laid = layout(stratum, tile_values, coords, counts, *sizes, done[-1])
        if stratum == strata - 1:
            return final(tile, u, row_half, cs, laid)
        axis = "group" if stratum == 2 else "blk"
        arrived, cs, done, residues = cs, [], [], []
        for h in range(CHUNKS):
            d, residue = columns(h, tile, row_half, arrived[h], laid)
            done.append(d)
            residues.append(residue)
            cs.append(shifted(d, axis))
        u, row_half = rows(u, residues, arrived)


def solution(mesh):
    return jax.shard_map(
        per_device,
        mesh=mesh,
        in_specs=(
            P(("blk", "group"), None),
            P(("blk", "group"), None),
            P(None, ("blk", "group"), None, None),
            P(None, ("blk", "group"), None),
            P(None, ("blk", "group")),
        ),
        out_specs=(P(("blk", "group"), None), P(("blk", "group"), None)),
        check_vma=False,
    )
```

```python
import functools

import jax
import jax.numpy as jnp
from jax import lax
from jax.experimental import pallas as pl
from jax.experimental.pallas import tpu as pltpu
from jax.sharding import PartitionSpec as P

LEARN_RATE = 0.03
DECAY_RATE = 0.1
CHUNKS = 2
SUBLANES = 8
EVEN, ODD = 0, 1

VMEM = pl.BlockSpec(memory_space=pltpu.VMEM)
SMEM = pl.BlockSpec(memory_space=pltpu.SMEM)
HBM = pl.BlockSpec(memory_space=pltpu.HBM)
ANY = pl.BlockSpec(memory_space=pl.ANY)


def call(body, name, operands, in_specs, outs, out_specs, flops=0, moved=0, aliases=None, scratch=()):
    return pl.pallas_call(
        body,
        out_shape=outs,
        in_specs=in_specs,
        out_specs=out_specs,
        input_output_aliases=aliases or {},
        scratch_shapes=list(scratch),
        compiler_params=pltpu.CompilerParams(vmem_limit_bytes=24 * 1024 * 1024),
        cost_estimate=pl.CostEstimate(flops=flops, bytes_accessed=moved, transcendentals=0),
        name=name,
    )(*operands)


class Line:
    def __init__(self, turn):
        self.turn = turn

    def call(self, body, name, operands, outs, flops=0, moved=0, aliases=None, held=()):
        through = (self.turn, *held)
        n_in, n_out, n_through = len(operands), len(outs), len(through)
        aliases = dict(aliases or {})
        for i in range(n_through):
            aliases[n_in + i] = n_out + i

        def inner(*refs):
            body(*refs[:n_in], *refs[n_in + n_through : n_in + n_through + n_out])

        out = call(
            inner,
            name,
            (*operands, *through),
            [VMEM] * (n_in + n_through),
            [*outs, *map(like, through)],
            [VMEM] * (n_out + n_through),
            flops,
            moved,
            aliases,
        )
        self.turn = out[n_out]
        return tuple(out[:n_out]) + tuple(out[n_out + 1 :])


def like(array, shape=None, dtype=None):
    return jax.ShapeDtypeStruct(shape or array.shape, dtype or array.dtype)


def span(h, width):
    return slice(h * width, (h + 1) * width)


def scatter(stratum, values, coords, counts, dense, live):
    listed, tile, _ = values.shape
    col = lax.broadcasted_iota(jnp.int32, live.shape, 0)
    row = lax.broadcasted_iota(jnp.int32, live.shape, 1)
    named = jnp.zeros(live.shape, jnp.float32)
    for t in range(listed):
        r = pl.multiple_of(coords[stratum, 0, t] * tile, tile)
        c = coords[stratum, 1, t]
        dense[pl.ds(pl.multiple_of(c * tile, tile), tile), pl.ds(r, tile)] = values[t].T
        alive_c = jnp.where(t < counts[0, stratum], c, -1)
        named = jnp.where((col == alive_c) & (row >= r) & (row < r + tile), 1.0, named)
    live[...] = named


def sgd(old, grad):
    return old + LEARN_RATE * (grad - DECAY_RATE * old)


def dot(a, b, contract):
    return lax.dot_general(a, b, (contract, ((), ())), preferred_element_type=jnp.float32)


def columns_step(first_tile, tile, row_half, cols, dense, live):
    col_half = cols.astype(jnp.bfloat16)
    estimate = dot(col_half, row_half, ((1,), (1,)))
    parts = []
    for i in range(cols.shape[0] // tile):
        at = span(i, tile)
        residue = dense[at].astype(jnp.float32) - estimate[at]
        named = live[first_tile + i : first_tile + i + 1] > 0
        parts.append(jnp.where(named, residue, 0.0).astype(jnp.bfloat16))
    residue = parts[0] if len(parts) == 1 else jnp.concatenate(parts, axis=0)
    return residue, col_half, sgd(cols, dot(residue, row_half, ((1,), (0,))))


def rows_gradient(residues, halves):
    return sum(dot(e[...], c[...], ((0,), (0,))) for e, c in zip(residues, halves))


def odd_device():
    return lax.axis_index("blk") % 2 == ODD


def when_parity(parity, body):
    if parity is None:
        body()
    else:
        pl.when(odd_device() == (parity == ODD))(body)


def first_kernel(u_hbm, c_hbm, x_hbm, coords_hbm, counts_hbm, *refs):
    u_ref, half_ref, col_half, residue, turn, whole = refs[:6]
    c_outs = refs[6 : 6 + CHUNKS]
    dense, live, c_ref, x_ref, coords, counts, sems = refs[6 + CHUNKS :]
    turn[...] = jnp.zeros_like(turn)
    tile = x_ref.shape[1]
    pairs = [(coords_hbm, coords), (counts_hbm, counts), (x_hbm.at[0], x_ref)]
    pairs += [(u_hbm, u_ref), (c_hbm, c_ref)]
    copies = [pltpu.make_async_copy(s, d, sems.at[i]) for i, (s, d) in enumerate(pairs)]
    for copy in copies:
        copy.start()
    for copy in copies[:3]:
        copy.wait()
    scatter(0, x_ref, coords, counts, dense, live)
    for copy in copies[3:]:
        copy.wait()
    row_half = u_ref[...].astype(jnp.bfloat16)
    half_ref[...] = row_half
    for h in range(CHUNKS):
        at = span(h, c_ref.shape[0] // CHUNKS)
        first_tile = at.start // tile
        residue[at], col_half[at], new = columns_step(
            first_tile, tile, row_half, c_ref[at], dense[at], live
        )
        c_outs[h][...] = new
        whole[at] = new


def first(u, c, values, coords, counts):
    rows, cols = u.shape[0], c.shape[0]
    part = (cols // CHUNKS, c.shape[1])
    halves = [like(u, dtype=jnp.bfloat16), like(c, dtype=jnp.bfloat16)]
    outs = [like(u), *halves, like(u, (cols, rows), jnp.bfloat16)]
    outs += [like(u, (SUBLANES, 128)), like(c)] + [like(c, part)] * CHUNKS
    operands = (u, c, values, coords, counts)
    return call(
        first_kernel,
        "first_columns",
        [pltpu.with_memory_space_constraint(x, pltpu.HBM) for x in operands],
        [HBM] * 5,
        outs,
        [VMEM] * len(outs),
        flops=4 * u.size * cols,
        moved=8 * u.size,
        scratch=[
            pltpu.VMEM((cols, rows), jnp.bfloat16),
            pltpu.VMEM((SUBLANES, rows), jnp.float32),
            pltpu.VMEM(c.shape, c.dtype),
            pltpu.VMEM(values.shape[1:], values.dtype),
            pltpu.SMEM(coords.shape, coords.dtype),
            pltpu.SMEM(counts.shape, counts.dtype),
            pltpu.SemaphoreType.DMA((5,)),
        ],
    )


def layout_kernel(x_ref, coords, counts, *refs):
    outs = refs[4:]
    later = len(outs) // 2
    for s in range(later):
        scatter(s + 1, x_ref.at[s + 1], coords, counts, outs[s], outs[later + s])


def layout(line, values, coords, counts, rows, cols, held):
    later = values.shape[0] - 1
    outs = [like(values, (cols, rows))] * later
    outs += [like(values, (SUBLANES, rows), jnp.float32)] * later
    line.turn, held, *out = call(
        layout_kernel,
        "lay_out_tiles",
        (values, coords, counts, line.turn, held),
        [VMEM, SMEM, SMEM, VMEM, VMEM],
        [like(line.turn), like(held), *outs],
        [VMEM] * (2 + len(outs)),
        moved=4 * later * rows * cols,
        aliases={3: 0, 4: 1},
    )
    return list(zip(out[:later], out[later:])), held


def choose(cs):
    return jnp.where(odd_device(), cs[ODD][...], cs[EVEN][...]) if len(cs) > 1 else cs[0][...]


def columns_kernel(h, tile, parity, row_half, dense, live, *refs):
    *cs, c_out, residue, col_half = refs

    def body():
        cols = choose(cs)
        at = span(h, cols.shape[0])
        residue[...], col_half[...], c_out[...] = columns_step(
            at.start // tile, tile, row_half[...], cols, dense[at], live
        )

    when_parity(parity, body)


def columns(line, h, tile, row_half, cs, laid, parity=None, held=()):
    c = cs[0]
    return line.call(
        functools.partial(columns_kernel, h, tile, parity),
        "columns_step",
        (row_half, *laid, *cs),
        [like(c), like(row_half, (c.shape[0], row_half.shape[0])), like(c, dtype=jnp.bfloat16)],
        flops=4 * row_half.size * c.shape[0],
        moved=2 * row_half.size + 8 * c.size,
        held=held,
    )


def rows_kernel(parity, _, __, *refs):
    *pairs, u_out, half_out = refs
    n = len(pairs) // 2

    def body():
        u_new = sgd(u_out[...], rows_gradient(pairs[:n], pairs[n:]))
        u_out[...] = u_new
        half_out[...] = u_new.astype(jnp.bfloat16)

    when_parity(parity, body)


def rows(line, u, row_half, residues, halves, parity=None, held=()):
    return line.call(
        functools.partial(rows_kernel, parity),
        "rows_step",
        (u, row_half, *residues, *halves),
        [like(u), like(row_half)],
        flops=2 * u.size * sum(c.shape[0] for c in halves),
        moved=10 * u.size,
        aliases={0: 0, 1: 1},
        held=held,
    )


def whole_kernel(tile, parity, _, __, dense, live, c_ref, u_out, half_out, *c_outs):
    def body():
        row_half = half_out[...]
        cols = c_ref[...]
        residue, col_half, new = columns_step(0, tile, row_half, cols, dense[...], live)
        for h, c_out in enumerate(c_outs):
            c_out[...] = new[span(h, c_out.shape[0])]
        u_new = sgd(u_out[...], dot(residue, col_half, ((0,), (0,))))
        u_out[...] = u_new
        half_out[...] = u_new.astype(jnp.bfloat16)

    when_parity(parity, body)


def whole_stratum(line, tile, u, row_half, c, laid, parity):
    u, row_half, *cs = line.call(
        functools.partial(whole_kernel, tile, parity),
        "whole_stratum",
        (u, row_half, *laid, c),
        [like(u), like(row_half)] + [like(c, (c.shape[0] // CHUNKS, c.shape[1]))] * CHUNKS,
        flops=6 * u.size * c.shape[0],
        moved=16 * u.size,
        aliases={0: 0, 1: 1},
    )
    return u, row_half, cs


def last_kernel(tile, u_ref, row_half, dense, live, even_c, odd_c, done, residue, half, _, u_hbm, c_hbm, u_new, c_new, sems):
    width = even_c.shape[0]
    h = c_hbm.shape[0] // width - 1
    copies = []

    def copy(source, target, at):
        place = pl.ds(at, source.shape[0])
        copies.append(pltpu.make_async_copy(source, target.at[place], sems.at[len(copies)]))
        copies[-1].start()

    copy(done, c_hbm, 0)
    last_residue, last_half, new_cols = columns_step(
        h * width // tile, tile, row_half[...], choose((even_c, odd_c)), dense[span(h, width)], live
    )
    for r in range(u_ref.shape[0] // tile):
        part = span(r, tile)
        grad = dot(residue[:, part], half[...], ((0,), (0,)))
        grad = grad + dot(last_residue[:, part], last_half, ((0,), (0,)))
        u_new[part] = sgd(u_ref[part], grad)
        copy(u_new.at[pl.ds(r * tile, tile)], u_hbm, r * tile)
    c_new[...] = new_cols
    copy(c_new, c_hbm, h * width)
    for started in copies:
        started.wait()


def final(line, tile, u, row_half, cs, laid):
    width, rank = cs[0][0].shape
    done, residue, half, held = columns(line, 0, tile, row_half, cs[0], laid, held=(cs[1][0],))
    return call(
        functools.partial(last_kernel, tile),
        "last_columns_and_rows",
        (u, row_half, *laid, held, cs[1][1], done, residue, half, line.turn),
        [VMEM] * 10,
        [like(u), like(u, (CHUNKS * width, rank))],
        [HBM, HBM],
        flops=6 * u.size * width,
        moved=8 * u.size,
        scratch=[
            pltpu.VMEM(u.shape, u.dtype),
            pltpu.VMEM((width, rank), u.dtype),
            pltpu.SemaphoreType.DMA((CHUNKS + u.shape[0] // tile,)),
        ],
    )


def ring(chunk):
    n = lax.axis_size("blk")
    return lax.ppermute(chunk, "blk", [(i, (i + 1) % n) for i in range(n)])


def swap(chunk):
    return lax.ppermute(chunk, "blk", [(i, i ^ 1) for i in range(lax.axis_size("blk"))])


def along_group(chunk, parity):
    blk, groups = lax.axis_size("blk"), lax.axis_size("group")
    route = []
    for b in range(blk):
        for g in range(groups):
            to = (g + 1) % groups if b % 2 == parity else g
            route.append((b * groups + g, b * groups + to))
    return lax.ppermute(chunk, ("blk", "group"), route)


def per_device(row_factors, col_factors, tile_values, tile_coords, tile_counts):
    tile = tile_values.shape[2]
    coords, counts = tile_coords.transpose(0, 2, 1), tile_counts.transpose(1, 0)
    sizes = row_factors.shape[0], col_factors.shape[0]
    u, row_half, half, residue, turn, whole, *done = first(
        row_factors, col_factors, tile_values, coords, counts
    )
    line = Line(turn)
    b1 = [ring(d) for d in done]
    laid, whole = layout(line, tile_values, coords, counts, *sizes, whole)
    a1 = swap(whole)
    step = functools.partial(columns, line)
    u, row_half = rows(line, u, row_half, [residue], [half])

    e1_0 = step(0, tile, row_half, b1[:1], laid[0], EVEN)
    a2_0 = swap(e1_0[0])
    u, row_half, o1 = whole_stratum(line, tile, u, row_half, a1, laid[0], ODD)
    b2 = [ring(d) for d in o1]
    e1_1 = step(1, tile, row_half, b1[1:], laid[0], EVEN)
    a2_1 = swap(e1_1[0])
    o2_0 = step(0, tile, row_half, (a2_0,), laid[1], ODD)
    zo_0 = along_group(o2_0[0], ODD)
    u, row_half = rows(line, u, row_half, (e1_0[1], e1_1[1]), (e1_0[2], e1_1[2]), EVEN)

    e2_0 = step(0, tile, row_half, b2[:1], laid[1], EVEN)
    ze_0 = along_group(e2_0[0], EVEN)
    o2_1 = step(1, tile, row_half, (a2_1,), laid[1], ODD)
    zo_1 = along_group(o2_1[0], ODD)
    u, row_half = rows(line, u, row_half, (o2_0[1], o2_1[1]), (o2_0[2], o2_1[2]), ODD)

    e2_1 = step(1, tile, row_half, b2[1:], laid[1], EVEN)
    ze_1 = along_group(e2_1[0], EVEN)
    o3_0 = step(0, tile, row_half, (zo_0,), laid[2], ODD)
    b4_0 = ring(o3_0[0])
    u, row_half = rows(line, u, row_half, (e2_0[1], e2_1[1]), (e2_0[2], e2_1[2]), EVEN)

    o3_1 = step(1, tile, row_half, (zo_1,), laid[2], ODD)
    b4_1 = ring(o3_1[0])
    u, row_half = rows(line, u, row_half, (o3_0[1], o3_1[1]), (o3_0[2], o3_1[2]), ODD)
    e3_0 = step(0, tile, row_half, (ze_0,), laid[2], EVEN)
    a4_0 = swap(e3_0[0])
    e3_1 = step(1, tile, row_half, (ze_1,), laid[2], EVEN)
    a4_1 = swap(e3_1[0])
    u, row_half = rows(line, u, row_half, (e3_0[1], e3_1[1]), (e3_0[2], e3_1[2]), EVEN)
    return final(line, tile, u, row_half, ((b4_0, a4_0), (b4_1, a4_1)), laid[3])


def solution(mesh):
    return jax.shard_map(
        per_device,
        mesh=mesh,
        in_specs=(
            P(("blk", "group"), None),
            P(("blk", "group"), None),
            P(None, ("blk", "group"), None, None),
            P(None, ("blk", "group"), None),
            P(None, ("blk", "group")),
        ),
        out_specs=(P(("blk", "group"), None), P(("blk", "group"), None)),
        check_vma=False,
    )
```

```python
import functools

import jax
import jax.numpy as jnp
from jax import lax
from jax.experimental import pallas as pl
from jax.experimental.pallas import tpu as pltpu
from jax.sharding import PartitionSpec as P

LEARN_RATE = 0.03
DECAY_RATE = 0.1
CHUNKS = 4
SUBLANES = 8

VMEM = pl.BlockSpec(memory_space=pltpu.VMEM)
SMEM = pl.BlockSpec(memory_space=pltpu.SMEM)
HBM = pl.BlockSpec(memory_space=pltpu.HBM)
ANY = pl.BlockSpec(memory_space=pl.ANY)


def call(body, name, operands, in_specs, outs, out_specs, flops=0, moved=0, aliases=None, scratch=()):
    return pl.pallas_call(
        body,
        out_shape=outs,
        in_specs=in_specs,
        out_specs=out_specs,
        input_output_aliases=aliases or {},
        scratch_shapes=list(scratch),
        compiler_params=pltpu.CompilerParams(vmem_limit_bytes=24 * 1024 * 1024),
        cost_estimate=pl.CostEstimate(flops=flops, bytes_accessed=moved, transcendentals=0),
        name=name,
    )(*operands)


class Line:
    def __init__(self, turn):
        self.turn = turn

    def call(self, body, name, operands, outs, flops=0, moved=0, aliases=None, held=()):
        through = (self.turn, *held)
        n_in, n_out, n_through = len(operands), len(outs), len(through)
        aliases = dict(aliases or {})
        for i in range(n_through):
            aliases[n_in + i] = n_out + i

        def inner(*refs):
            body(*refs[:n_in], *refs[n_in + n_through : n_in + n_through + n_out])

        out = call(
            inner,
            name,
            (*operands, *through),
            [VMEM] * (n_in + n_through),
            [*outs, *map(like, through)],
            [VMEM] * (n_out + n_through),
            flops,
            moved,
            aliases,
        )
        self.turn = out[n_out]
        return tuple(out[:n_out]) + tuple(out[n_out + 1 :])


def like(array, shape=None, dtype=None):
    return jax.ShapeDtypeStruct(shape or array.shape, dtype or array.dtype)


def span(h, width):
    return slice(h * width, (h + 1) * width)


def scatter(stratum, values, coords, counts, dense, live):
    listed, tile, _ = values.shape
    col = lax.broadcasted_iota(jnp.int32, live.shape, 0)
    row = lax.broadcasted_iota(jnp.int32, live.shape, 1)
    named = jnp.zeros(live.shape, jnp.float32)
    for t in range(listed):
        r = pl.multiple_of(coords[stratum, 0, t] * tile, tile)
        c = coords[stratum, 1, t]
        dense[pl.ds(pl.multiple_of(c * tile, tile), tile), pl.ds(r, tile)] = values[t].T
        alive_c = jnp.where(t < counts[0, stratum], c, -1)
        named = jnp.where((col == alive_c) & (row >= r) & (row < r + tile), 1.0, named)
    live[...] = named


def sgd(old, grad):
    return old + LEARN_RATE * (grad - DECAY_RATE * old)


def dot(a, b, contract):
    return lax.dot_general(a, b, (contract, ((), ())), preferred_element_type=jnp.float32)


def columns_step(first_tile, tile, row_half, cols, dense, live):
    col_half = cols.astype(jnp.bfloat16)
    estimate = dot(col_half, row_half, ((1,), (1,)))
    parts = []
    for i in range(cols.shape[0] // tile):
        at = span(i, tile)
        residue = dense[at].astype(jnp.float32) - estimate[at]
        named = live[first_tile + i : first_tile + i + 1] > 0
        parts.append(jnp.where(named, residue, 0.0).astype(jnp.bfloat16))
    residue = parts[0] if len(parts) == 1 else jnp.concatenate(parts, axis=0)
    return residue, col_half, sgd(cols, dot(residue, row_half, ((1,), (0,))))


def rows_gradient(residues, halves):
    return sum(dot(e[...], c[...], ((0,), (0,))) for e, c in zip(residues, halves))


def first_kernel(u_hbm, c_hbm, x_hbm, coords_hbm, counts_hbm, *refs):
    u_ref, c_ref, half_ref, dense, live, turn, c_out, residue, col_half = refs[:9]
    x_ref, coords, counts, sems = refs[9:]
    width, tile = c_out.shape[0], x_ref.shape[1]
    cols = c_ref.shape[0]
    head, tail = pl.ds(0, width), pl.ds(width, cols - width)
    pairs = [(coords_hbm, coords), (counts_hbm, counts), (x_hbm.at[0], x_ref), (u_hbm, u_ref)]
    pairs += [(c_hbm.at[at], c_ref.at[at]) for at in (head, tail)]
    copies = [pltpu.make_async_copy(s, d, sems.at[i]) for i, (s, d) in enumerate(pairs)]
    for copy in copies:
        copy.start()
    turn[...] = jnp.zeros_like(turn)
    for copy in copies[:3]:
        copy.wait()
    scatter(0, x_ref, coords, counts, dense, live)
    copies[3].wait()
    row_half = u_ref[...].astype(jnp.bfloat16)
    half_ref[...] = row_half
    copies[4].wait()
    residue[...], col_half[...], c_out[...] = columns_step(
        0, tile, row_half, c_ref[:width], dense[:width], live
    )
    copies[5].wait()


def first(u, c, values, coords, counts):
    rows, cols = u.shape[0], c.shape[0]
    part = (cols // CHUNKS, c.shape[1])
    bf16 = jnp.bfloat16
    outs = [like(u), like(c), like(u, dtype=bf16), like(u, (cols, rows), bf16)]
    outs += [like(u, (SUBLANES, rows)), like(u, (SUBLANES, 128))]
    outs += [like(c, part), like(u, (part[0], rows), bf16), like(c, part, bf16)]
    operands = (u, c, values, coords, counts)
    return call(
        first_kernel,
        "first_chunk",
        [pltpu.with_memory_space_constraint(x, pltpu.HBM) for x in operands],
        [HBM] * 5,
        outs,
        [VMEM] * len(outs),
        flops=4 * u.size * part[0],
        moved=8 * u.size,
        scratch=[
            pltpu.VMEM(values.shape[1:], values.dtype),
            pltpu.SMEM(coords.shape, coords.dtype),
            pltpu.SMEM(counts.shape, counts.dtype),
            pltpu.SemaphoreType.DMA((6,)),
        ],
    )


def other_kernel(tile, row_half, c_ref, dense, live, residue, col_half, *c_outs):
    width = c_outs[0].shape[0]
    rest = slice(width, c_ref.shape[0])
    residue[...], col_half[...], new = columns_step(
        width // tile, tile, row_half[...], c_ref[rest], dense[rest], live
    )
    for h, c_out in enumerate(c_outs):
        c_out[...] = new[span(h, width)]


def others(line, tile, row_half, c, laid):
    cols, rank = c.shape
    width = cols // CHUNKS
    outs = [like(row_half, (cols - width, row_half.shape[0])), like(row_half, (cols - width, rank))]
    return line.call(
        functools.partial(other_kernel, tile),
        "other_chunks",
        (row_half, c, *laid),
        outs + [like(c, (width, rank))] * (CHUNKS - 1),
        flops=4 * row_half.size * (cols - width),
        moved=8 * c.size,
    )


def layout_kernel(x_ref, coords, counts, *refs):
    outs = refs[2:]
    later = len(outs) // 2
    for s in range(later):
        scatter(s + 1, x_ref.at[s + 1], coords, counts, outs[s], outs[later + s])


def layout(line, values, coords, counts, rows, cols):
    later = values.shape[0] - 1
    outs = [like(values, (cols, rows))] * later
    outs += [like(values, (SUBLANES, rows), jnp.float32)] * later
    line.turn, *out = call(
        layout_kernel,
        "lay_out_tiles",
        (values, coords, counts, line.turn),
        [VMEM, SMEM, SMEM, VMEM],
        [like(line.turn), *outs],
        [VMEM] * (1 + len(outs)),
        moved=4 * later * rows * cols,
        aliases={3: 0},
    )
    return list(zip(out[:later], out[later:]))


def columns_kernel(h, tile, row_half, c_ref, dense, live, c_out, residue, col_half):
    at = span(h, c_ref.shape[0])
    residue[...], col_half[...], c_out[...] = columns_step(
        at.start // tile, tile, row_half[...], c_ref[...], dense[at], live
    )


def columns(line, h, tile, row_half, c, laid, held=()):
    return line.call(
        functools.partial(columns_kernel, h, tile),
        "columns_step",
        (row_half, c, *laid),
        [like(c), like(row_half, (c.shape[0], row_half.shape[0])), like(c, dtype=jnp.bfloat16)],
        flops=4 * row_half.size * c.shape[0],
        moved=2 * row_half.size + 8 * c.size,
        held=held,
    )


def rows_kernel(_, __, *refs):
    *pairs, u_out, half_out = refs
    n = len(pairs) // 2
    u_new = sgd(u_out[...], rows_gradient(pairs[:n], pairs[n:]))
    u_out[...] = u_new
    half_out[...] = u_new.astype(jnp.bfloat16)


def rows(line, u, row_half, residues, halves):
    return line.call(
        rows_kernel,
        "rows_step",
        (u, row_half, *residues, *halves),
        [like(u), like(row_half)],
        flops=2 * u.size * sum(c.shape[0] for c in halves),
        moved=10 * u.size,
        aliases={0: 0, 1: 1},
    )


def gradient_kernel(*refs):
    *pairs, acc = refs
    n = len(pairs) // 2
    acc[...] = rows_gradient(pairs[:n], pairs[n:])


def last_kernel(tile, u_ref, row_half, dense, live, c_ref, acc, _, *refs):
    n = CHUNKS - 1
    done, (u_hbm, c_hbm, u_new, c_new, sems) = refs[:n], refs[n:]
    width = c_ref.shape[0]
    copies = []

    def copy(source, target, at):
        place = pl.ds(at, source.shape[0])
        copies.append(pltpu.make_async_copy(source, target.at[place], sems.at[len(copies)]))
        copies[-1].start()

    for h, c in enumerate(done):
        copy(c, c_hbm, h * width)
    residue, col_half, new_cols = columns_step(
        n * width // tile, tile, row_half[...], c_ref[...], dense[span(n, width)], live
    )
    for r in range(u_ref.shape[0] // tile):
        part = span(r, tile)
        grad = acc[part] + dot(residue[:, part], col_half, ((0,), (0,)))
        u_new[part] = sgd(u_ref[part], grad)
        copy(u_new.at[pl.ds(r * tile, tile)], u_hbm, r * tile)
    c_new[...] = new_cols
    copy(c_new, c_hbm, n * width)
    for started in copies:
        started.wait()


def final(line, tile, u, row_half, cs, laid):
    n = CHUNKS - 1
    width, rank = cs[0].shape
    steps = [columns(line, h, tile, row_half, cs[h], laid) for h in range(n)]
    done, residues, halves = zip(*steps)
    (acc,) = line.call(
        gradient_kernel,
        "rows_gradient",
        (*residues, *halves),
        [like(u)],
        flops=2 * u.size * n * width,
        moved=4 * u.size,
    )
    return call(
        functools.partial(last_kernel, tile),
        "last_columns_and_rows",
        (u, row_half, *laid, cs[n], acc, line.turn, *done),
        [VMEM] * (7 + n),
        [like(u), like(u, (CHUNKS * width, rank))],
        [HBM, HBM],
        flops=6 * u.size * width,
        moved=8 * u.size,
        scratch=[
            pltpu.VMEM(u.shape, u.dtype),
            pltpu.VMEM((width, rank), u.dtype),
            pltpu.SemaphoreType.DMA((CHUNKS + u.shape[0] // tile,)),
        ],
    )


def shifted(chunk, axis):
    n = lax.axis_size(axis)
    return lax.ppermute(chunk, axis, [(i, (i + 1) % n) for i in range(n)])


def per_device(row_factors, col_factors, tile_values, tile_coords, tile_counts):
    tile = tile_values.shape[2]
    strata = tile_values.shape[0]
    coords, counts = tile_coords.transpose(0, 2, 1), tile_counts.transpose(1, 0)
    sizes = row_factors.shape[0], col_factors.shape[0]
    u, c, row_half, *laid0, turn, done, residue, half = first(
        row_factors, col_factors, tile_values, coords, counts
    )
    line = Line(turn)
    cs = [shifted(done, "blk")]
    residues, halves, *done = others(line, tile, row_half, c, laid0)
    cs += [shifted(d, "blk") for d in done]
    laid = layout(line, tile_values, coords, counts, *sizes)
    u, row_half = rows(line, u, row_half, (residue, residues), (half, halves))

    waiting = []
    for stratum in range(1, strata - 1):
        axis = "group" if stratum == 2 else "blk"
        arrived, cs, residues, halves = cs, [], [], []
        for h in range(CHUNKS):
            held = tuple(waiting) if h == 1 else ()
            done, residue, half, *held = columns(
                line, h, tile, row_half, arrived[h], laid[stratum - 1], held
            )
            residues.append(residue)
            halves.append(half)
            cs.append(shifted(done, axis) if stratum != 1 or h + 1 < CHUNKS else done)
            for d in held:
                arrived[CHUNKS - 1] = shifted(d, "blk")
        waiting = cs[-1:] if stratum == 1 else []
        u, row_half = rows(line, u, row_half, residues, halves)
    return final(line, tile, u, row_half, cs, laid[-1])


def solution(mesh):
    return jax.shard_map(
        per_device,
        mesh=mesh,
        in_specs=(
            P(("blk", "group"), None),
            P(("blk", "group"), None),
            P(None, ("blk", "group"), None, None),
            P(None, ("blk", "group"), None),
            P(None, ("blk", "group")),
        ),
        out_specs=(P(("blk", "group"), None), P(("blk", "group"), None)),
        check_vma=False,
    )
```

```python
import functools

import jax
import jax.numpy as jnp
from jax import lax
from jax.experimental import pallas as pl
from jax.experimental.pallas import tpu as pltpu
from jax.sharding import PartitionSpec as P

LEARN_RATE = 0.03
DECAY_RATE = 0.1
EDGES = (0, 3, 8, 13, 16)
CHUNKS = len(EDGES) - 1
WEIGHTS = (10**9, 10**7, 6 * 10**8, 2 * 10**9)
SUBLANES = 8

VMEM = pl.BlockSpec(memory_space=pltpu.VMEM)
SMEM = pl.BlockSpec(memory_space=pltpu.SMEM)
HBM = pl.BlockSpec(memory_space=pltpu.HBM)
ANY = pl.BlockSpec(memory_space=pl.ANY)


def call(body, name, operands, in_specs, outs, out_specs, flops=10**7, aliases=None, scratch=()):
    return pl.pallas_call(
        body,
        out_shape=outs,
        in_specs=in_specs,
        out_specs=out_specs,
        input_output_aliases=aliases or {},
        scratch_shapes=list(scratch),
        compiler_params=pltpu.CompilerParams(vmem_limit_bytes=24 * 1024 * 1024),
        cost_estimate=pl.CostEstimate(flops=flops, bytes_accessed=1, transcendentals=0),
        name=name,
    )(*operands)


class Line:
    def __init__(self, turn):
        self.turn = turn

    def call(self, body, name, operands, outs, flops=10**7, aliases=None):
        n_in = len(operands)

        def inner(*refs):
            body(*refs[:n_in], *refs[n_in + 2 :])

        self.turn, *out = call(
            inner,
            name,
            (*operands, self.turn),
            [VMEM] * (n_in + 1),
            [like(self.turn), *outs],
            [VMEM] * (1 + len(outs)),
            flops,
            {n_in: 0, **{i: o + 1 for i, o in (aliases or {}).items()}},
        )
        return out


def like(array, shape=None, dtype=None):
    return jax.ShapeDtypeStruct(shape or array.shape, dtype or array.dtype)


def span(h, width):
    return slice(h * width, (h + 1) * width)


def chunk_span(h, cols):
    return slice(cols * EDGES[h] // 16, cols * EDGES[h + 1] // 16)


def chunk_width(h, cols):
    at = chunk_span(h, cols)
    return at.stop - at.start


def scatter(stratum, values, coords, counts, dense, live):
    listed, tile, _ = values.shape
    col = lax.broadcasted_iota(jnp.int32, live.shape, 0)
    row = lax.broadcasted_iota(jnp.int32, live.shape, 1)
    named = jnp.zeros(live.shape, jnp.float32)
    for t in range(listed):
        r = pl.multiple_of(coords[stratum, 0, t] * tile, tile)
        c = coords[stratum, 1, t]
        dense[pl.ds(pl.multiple_of(c * tile, tile), tile), pl.ds(r, tile)] = values[t].T
        alive_c = jnp.where(t < counts[0, stratum], c, -1)
        named = jnp.where((col == alive_c) & (row >= r) & (row < r + tile), 1.0, named)
    live[...] = named


def sgd(old, grad):
    return old + LEARN_RATE * (grad - DECAY_RATE * old)


def dot(a, b, contract):
    return lax.dot_general(a, b, (contract, ((), ())), preferred_element_type=jnp.float32)


def columns_step(start, tile, row_half, cols, dense, live):
    col_half = cols.astype(jnp.bfloat16)
    estimate = dot(col_half, row_half, ((1,), (1,)))
    parts, at, stop = [], start, start + cols.shape[0]
    while at < stop:
        c = at // tile
        end = min((c + 1) * tile, stop)
        here = slice(at - start, end - start)
        residue = dense[here].astype(jnp.float32) - estimate[here]
        parts.append(jnp.where(live[c : c + 1] > 0, residue, 0.0).astype(jnp.bfloat16))
        at = end
    residue = parts[0] if len(parts) == 1 else jnp.concatenate(parts, axis=0)
    return residue, col_half, sgd(cols, dot(residue, row_half, ((1,), (0,))))


def rows_gradient(residues, halves):
    return sum(dot(e[...], c[...], ((0,), (0,))) for e, c in zip(residues, halves))


def first_kernel(u_hbm, c_hbm, x_hbm, coords_hbm, counts_hbm, *refs):
    u_ref, c_ref, half_ref, dense, live, turn, c_out, residue, col_half = refs[:9]
    x_ref, coords, counts, sems = refs[9:]
    width, tile = c_out.shape[0], x_ref.shape[1]
    cols = c_ref.shape[0]
    head, tail = pl.ds(0, width), pl.ds(width, cols - width)
    pairs = [(coords_hbm, coords), (counts_hbm, counts), (x_hbm.at[0], x_ref), (u_hbm, u_ref)]
    pairs += [(c_hbm.at[at], c_ref.at[at]) for at in (head, tail)]
    copies = [pltpu.make_async_copy(s, d, sems.at[i]) for i, (s, d) in enumerate(pairs)]
    for copy in copies:
        copy.start()
    turn[...] = jnp.zeros_like(turn)
    for copy in copies[:3]:
        copy.wait()
    scatter(0, x_ref, coords, counts, dense, live)
    copies[3].wait()
    row_half = u_ref[...].astype(jnp.bfloat16)
    half_ref[...] = row_half
    copies[4].wait()
    residue[...], col_half[...], c_out[...] = columns_step(
        0, tile, row_half, c_ref[:width], dense[:width], live
    )
    copies[5].wait()


def first(u, c, values, coords, counts):
    rows, cols = u.shape[0], c.shape[0]
    part = (chunk_width(0, cols), c.shape[1])
    bf16 = jnp.bfloat16
    outs = [like(u), like(c), like(u, dtype=bf16), like(u, (cols, rows), bf16)]
    outs += [like(u, (SUBLANES, rows)), like(u, (SUBLANES, 128))]
    outs += [like(c, part), like(u, (part[0], rows), bf16), like(c, part, bf16)]
    operands = (u, c, values, coords, counts)
    return call(
        first_kernel,
        "first_chunk",
        [pltpu.with_memory_space_constraint(x, pltpu.HBM) for x in operands],
        [HBM] * 5,
        outs,
        [VMEM] * len(outs),
        scratch=[
            pltpu.VMEM(values.shape[1:], values.dtype),
            pltpu.SMEM(coords.shape, coords.dtype),
            pltpu.SMEM(counts.shape, counts.dtype),
            pltpu.SemaphoreType.DMA((6,)),
        ],
    )


def other_kernel(tile, row_half, c_ref, dense, live, residue, col_half, *c_outs):
    start, cols = c_ref.shape[0] - residue.shape[0], c_ref.shape[0]
    rest = slice(start, cols)
    residue[...], col_half[...], new = columns_step(
        start, tile, row_half[...], c_ref[rest], dense[rest], live
    )
    for h, c_out in enumerate(c_outs, 1):
        at = chunk_span(h, cols)
        c_out[...] = new[at.start - start : at.stop - start]


def others(line, tile, row_half, c, laid):
    cols, rank = c.shape
    rest = cols - chunk_width(0, cols)
    outs = [like(row_half, (rest, row_half.shape[0])), like(row_half, (rest, rank))]
    return line.call(
        functools.partial(other_kernel, tile),
        "other_chunks",
        (row_half, c, *laid),
        outs + [like(c, (chunk_width(h, cols), rank)) for h in range(1, CHUNKS)],
    )


def layout_kernel(x_ref, coords, counts, *refs):
    outs = refs[2:]
    later = len(outs) // 2
    for s in range(later):
        scatter(s + 1, x_ref.at[s + 1], coords, counts, outs[s], outs[later + s])


def layout(line, values, coords, counts, rows, cols):
    later = values.shape[0] - 1
    outs = [like(values, (cols, rows))] * later
    outs += [like(values, (SUBLANES, rows), jnp.float32)] * later
    line.turn, *out = call(
        layout_kernel,
        "lay_out_tiles",
        (values, coords, counts, line.turn),
        [VMEM, SMEM, SMEM, VMEM],
        [like(line.turn), *outs],
        [VMEM] * (1 + len(outs)),
        aliases={3: 0},
    )
    return list(zip(out[:later], out[later:]))


def columns_kernel(h, tile, row_half, c_ref, dense, live, c_out, residue, col_half):
    at = chunk_span(h, dense.shape[0])
    residue[...], col_half[...], c_out[...] = columns_step(
        at.start, tile, row_half[...], c_ref[...], dense[at], live
    )


def columns(line, h, tile, row_half, c, laid):
    return line.call(
        functools.partial(columns_kernel, h, tile),
        "columns_step",
        (row_half, c, *laid),
        [like(c), like(row_half, (c.shape[0], row_half.shape[0])), like(c, dtype=jnp.bfloat16)],
        flops=WEIGHTS[h],
    )


def rows_kernel(_, __, *refs):
    *pairs, u_out, half_out = refs
    n = len(pairs) // 2
    u_new = sgd(u_out[...], rows_gradient(pairs[:n], pairs[n:]))
    u_out[...] = u_new
    half_out[...] = u_new.astype(jnp.bfloat16)


def rows(line, u, row_half, residues, halves):
    return line.call(
        rows_kernel,
        "rows_step",
        (u, row_half, *residues, *halves),
        [like(u), like(row_half)],
        aliases={0: 0, 1: 1},
    )


def gradient_kernel(*refs):
    *pairs, acc = refs
    n = len(pairs) // 2
    acc[...] = rows_gradient(pairs[:n], pairs[n:])


def last_kernel(tile, u_ref, row_half, dense, live, c_ref, acc, _, *refs):
    n = CHUNKS - 1
    done, (u_hbm, c_hbm, u_new, c_new, sems) = refs[:n], refs[n:]
    cols = c_hbm.shape[0]
    copies = []

    def copy(source, target, at):
        place = pl.ds(at, source.shape[0])
        copies.append(pltpu.make_async_copy(source, target.at[place], sems.at[len(copies)]))
        copies[-1].start()

    for h, c in enumerate(done):
        copy(c, c_hbm, chunk_span(h, cols).start)
    at = chunk_span(n, cols)
    residue, col_half, new_cols = columns_step(
        at.start, tile, row_half[...], c_ref[...], dense[at], live
    )
    for r in range(u_ref.shape[0] // tile):
        part = span(r, tile)
        grad = acc[part] + dot(residue[:, part], col_half, ((0,), (0,)))
        u_new[part] = sgd(u_ref[part], grad)
        copy(u_new.at[pl.ds(r * tile, tile)], u_hbm, r * tile)
    c_new[...] = new_cols
    copy(c_new, c_hbm, at.start)
    for started in copies:
        started.wait()


def final(line, tile, u, row_half, cs, laid):
    n = CHUNKS - 1
    cols, rank = laid[0].shape[0], u.shape[1]
    steps = [columns(line, h, tile, row_half, cs[h], laid) for h in range(n)]
    done, residues, halves = zip(*steps)
    (acc,) = line.call(
        gradient_kernel,
        "rows_gradient",
        (*residues, *halves),
        [like(u)],
    )
    return call(
        functools.partial(last_kernel, tile),
        "last_columns_and_rows",
        (u, row_half, *laid, cs[n], acc, line.turn, *done),
        [VMEM] * (7 + n),
        [like(u), like(u, (cols, rank))],
        [HBM, HBM],
        scratch=[
            pltpu.VMEM(u.shape, u.dtype),
            pltpu.VMEM(cs[n].shape, u.dtype),
            pltpu.SemaphoreType.DMA((CHUNKS + u.shape[0] // tile,)),
        ],
    )


def shifted(chunk, axis):
    n = lax.axis_size(axis)
    return lax.ppermute(chunk, axis, [(i, (i + 1) % n) for i in range(n)])


def per_device(row_factors, col_factors, tile_values, tile_coords, tile_counts):
    tile = tile_values.shape[2]
    strata = tile_values.shape[0]
    coords, counts = tile_coords.transpose(0, 2, 1), tile_counts.transpose(1, 0)
    sizes = row_factors.shape[0], col_factors.shape[0]
    u, c, row_half, *laid0, turn, done, residue, half = first(
        row_factors, col_factors, tile_values, coords, counts
    )
    line = Line(turn)
    cs = [shifted(done, "blk")]
    residues, halves, *done = others(line, tile, row_half, c, laid0)
    cs += [shifted(d, "blk") for d in done]
    laid = layout(line, tile_values, coords, counts, *sizes)
    u, row_half = rows(line, u, row_half, (residue, residues), (half, halves))

    for stratum in range(1, strata - 1):
        axis = "group" if stratum == 2 else "blk"
        arrived, cs, residues, halves = cs, [], [], []
        for h in range(CHUNKS):
            done, residue, half = columns(line, h, tile, row_half, arrived[h], laid[stratum - 1])
            cs.append(shifted(done, axis))
            residues.append(residue)
            halves.append(half)
        u, row_half = rows(line, u, row_half, residues, halves)
    return final(line, tile, u, row_half, cs, laid[-1])


def solution(mesh):
    return jax.shard_map(
        per_device,
        mesh=mesh,
        in_specs=(
            P(("blk", "group"), None),
            P(("blk", "group"), None),
            P(None, ("blk", "group"), None, None),
            P(None, ("blk", "group"), None),
            P(None, ("blk", "group")),
        ),
        out_specs=(P(("blk", "group"), None), P(("blk", "group"), None)),
        check_vma=False,
    )
```

```python
import functools

import jax
import jax.numpy as jnp
from jax import lax
from jax.experimental import pallas as pl
from jax.experimental.pallas import tpu as pltpu
from jax.sharding import PartitionSpec as P

LEARN_RATE = 0.03
DECAY_RATE = 0.1
EDGES = (0, 3, 8, 13, 16)
CHUNKS = len(EDGES) - 1
WEIGHTS = (10**9, 10**7, 6 * 10**8, 2 * 10**9)
SUBLANES = 8

VMEM = pl.BlockSpec(memory_space=pltpu.VMEM)
SMEM = pl.BlockSpec(memory_space=pltpu.SMEM)
HBM = pl.BlockSpec(memory_space=pltpu.HBM)
ANY = pl.BlockSpec(memory_space=pl.ANY)


def call(body, name, operands, in_specs, outs, out_specs, flops=10**7, aliases=None, scratch=()):
    return pl.pallas_call(
        body,
        out_shape=outs,
        in_specs=in_specs,
        out_specs=out_specs,
        input_output_aliases=aliases or {},
        scratch_shapes=list(scratch),
        compiler_params=pltpu.CompilerParams(vmem_limit_bytes=24 * 1024 * 1024),
        cost_estimate=pl.CostEstimate(flops=flops, bytes_accessed=1, transcendentals=0),
        name=name,
    )(*operands)


class Line:
    def __init__(self, turn):
        self.turn = turn

    def call(self, body, name, operands, outs, flops=10**7, aliases=None):
        n_in = len(operands)

        def inner(*refs):
            body(*refs[:n_in], *refs[n_in + 2 :])

        self.turn, *out = call(
            inner,
            name,
            (*operands, self.turn),
            [VMEM] * (n_in + 1),
            [like(self.turn), *outs],
            [VMEM] * (1 + len(outs)),
            flops,
            {n_in: 0, **{i: o + 1 for i, o in (aliases or {}).items()}},
        )
        return out


def like(array, shape=None, dtype=None):
    return jax.ShapeDtypeStruct(shape or array.shape, dtype or array.dtype)


def span(h, width):
    return slice(h * width, (h + 1) * width)


def chunk_span(h, cols):
    return slice(cols * EDGES[h] // 16, cols * EDGES[h + 1] // 16)


def chunk_width(h, cols):
    at = chunk_span(h, cols)
    return at.stop - at.start


def scatter(stratum, values, coords, counts, dense, live):
    listed, tile, _ = values.shape
    col = lax.broadcasted_iota(jnp.int32, live.shape, 0)
    row = lax.broadcasted_iota(jnp.int32, live.shape, 1)
    named = jnp.zeros(live.shape, jnp.float32)
    for t in range(listed):
        r = pl.multiple_of(coords[stratum, 0, t] * tile, tile)
        c = coords[stratum, 1, t]
        dense[pl.ds(pl.multiple_of(c * tile, tile), tile), pl.ds(r, tile)] = values[t].T
        alive_c = jnp.where(t < counts[0, stratum], c, -1)
        named = jnp.where((col == alive_c) & (row >= r) & (row < r + tile), 1.0, named)
    live[...] = named


def sgd(old, grad):
    return old + LEARN_RATE * (grad - DECAY_RATE * old)


def dot(a, b, contract):
    return lax.dot_general(a, b, (contract, ((), ())), preferred_element_type=jnp.float32)


def residue_of(start, tile, row_half, col_half, dense, live):
    estimate = dot(col_half, row_half, ((1,), (1,)))
    parts, at, stop = [], start, start + col_half.shape[0]
    while at < stop:
        c = at // tile
        end = min((c + 1) * tile, stop)
        here = slice(at - start, end - start)
        residue = dense[here].astype(jnp.float32) - estimate[here]
        parts.append(jnp.where(live[c : c + 1] > 0, residue, 0.0).astype(jnp.bfloat16))
        at = end
    return parts[0] if len(parts) == 1 else jnp.concatenate(parts, axis=0)


def columns_step(start, tile, row_half, cols, dense, live):
    col_half = cols.astype(jnp.bfloat16)
    residue = residue_of(start, tile, row_half, col_half, dense, live)
    return residue, col_half, sgd(cols, dot(residue, row_half, ((1,), (0,))))


def rows_gradient(residues, halves):
    return sum(dot(e[...], c[...], ((0,), (0,))) for e, c in zip(residues, halves))


def first_kernel(u_hbm, c_hbm, x_hbm, coords_hbm, counts_hbm, *refs):
    u_ref, c_ref, half_ref, dense, live, turn, c_out, residue, col_half = refs[:9]
    x_ref, coords, counts, sems = refs[9:]
    width, tile = c_out.shape[0], x_ref.shape[1]
    cols = c_ref.shape[0]
    head, tail = pl.ds(0, width), pl.ds(width, cols - width)
    pairs = [(coords_hbm, coords), (counts_hbm, counts), (x_hbm.at[0], x_ref), (u_hbm, u_ref)]
    pairs += [(c_hbm.at[at], c_ref.at[at]) for at in (head, tail)]
    copies = [pltpu.make_async_copy(s, d, sems.at[i]) for i, (s, d) in enumerate(pairs)]
    for copy in copies[:5]:
        copy.start()
    turn[...] = jnp.zeros_like(turn)
    for copy in copies[:3]:
        copy.wait()
    copies[5].start()
    scatter(0, x_ref, coords, counts, dense, live)
    copies[3].wait()
    row_half = u_ref[...].astype(jnp.bfloat16)
    half_ref[...] = row_half
    copies[4].wait()
    residue[...], col_half[...], c_out[...] = columns_step(
        0, tile, row_half, c_ref[:width], dense[:width], live
    )
    copies[5].wait()


def first(u, c, values, coords, counts):
    rows, cols = u.shape[0], c.shape[0]
    part = (chunk_width(0, cols), c.shape[1])
    bf16 = jnp.bfloat16
    outs = [like(u), like(c), like(u, dtype=bf16), like(u, (cols, rows), bf16)]
    outs += [like(u, (SUBLANES, rows)), like(u, (SUBLANES, 128))]
    outs += [like(c, part), like(u, (part[0], rows), bf16), like(c, part, bf16)]
    operands = (u, c, values, coords, counts)
    return call(
        first_kernel,
        "first_chunk",
        [pltpu.with_memory_space_constraint(x, pltpu.HBM) for x in operands],
        [HBM] * 5,
        outs,
        [VMEM] * len(outs),
        scratch=[
            pltpu.VMEM(values.shape[1:], values.dtype),
            pltpu.SMEM(coords.shape, coords.dtype),
            pltpu.SMEM(counts.shape, counts.dtype),
            pltpu.SemaphoreType.DMA((6,)),
        ],
    )


def other_kernel(tile, row_half, c_ref, dense, live, residue, col_half, *c_outs):
    start, cols = c_ref.shape[0] - residue.shape[0], c_ref.shape[0]
    rest = slice(start, cols)
    residue[...], col_half[...], new = columns_step(
        start, tile, row_half[...], c_ref[rest], dense[rest], live
    )
    for h, c_out in enumerate(c_outs, 1):
        at = chunk_span(h, cols)
        c_out[...] = new[at.start - start : at.stop - start]


def others(line, tile, row_half, c, laid):
    cols, rank = c.shape
    rest = cols - chunk_width(0, cols)
    outs = [like(row_half, (rest, row_half.shape[0])), like(row_half, (rest, rank))]
    return line.call(
        functools.partial(other_kernel, tile),
        "other_chunks",
        (row_half, c, *laid),
        outs + [like(c, (chunk_width(h, cols), rank)) for h in range(1, CHUNKS)],
    )


def layout_kernel(x_ref, coords, counts, *refs):
    outs = refs[2:]
    later = len(outs) // 2
    for s in range(later):
        scatter(s + 1, x_ref.at[s + 1], coords, counts, outs[s], outs[later + s])


def layout(line, values, coords, counts, rows, cols):
    later = values.shape[0] - 1
    outs = [like(values, (cols, rows))] * later
    outs += [like(values, (SUBLANES, rows), jnp.float32)] * later
    line.turn, *out = call(
        layout_kernel,
        "lay_out_tiles",
        (values, coords, counts, line.turn),
        [VMEM, SMEM, SMEM, VMEM],
        [like(line.turn), *outs],
        [VMEM] * (1 + len(outs)),
        aliases={3: 0},
    )
    return list(zip(out[:later], out[later:]))


def columns_kernel(h, tile, row_half, c_ref, dense, live, c_out, residue, col_half):
    at = chunk_span(h, dense.shape[0])
    residue[...], col_half[...], c_out[...] = columns_step(
        at.start, tile, row_half[...], c_ref[...], dense[at], live
    )


def columns(line, h, tile, row_half, c, laid):
    return line.call(
        functools.partial(columns_kernel, h, tile),
        "columns_step",
        (row_half, c, *laid),
        [like(c), like(row_half, (c.shape[0], row_half.shape[0])), like(c, dtype=jnp.bfloat16)],
        flops=WEIGHTS[h],
    )


def gradient_kernel(*refs):
    *pairs, acc = refs
    n = len(pairs) // 2
    acc[...] = rows_gradient(pairs[:n], pairs[n:])


def gradient(line, u, residues, halves):
    (acc,) = line.call(gradient_kernel, "rows_gradient", (*residues, *halves), [like(u)])
    return acc


def rows_kernel(part, _, __, *refs):
    *pairs, u_out, half_out = refs
    before, pairs = pairs[:part], pairs[part:]
    n = len(pairs) // 2
    grad = rows_gradient(pairs[:n], pairs[n:])
    for acc in before:
        grad = grad + acc[...]
    u_new = sgd(u_out[...], grad)
    u_out[...] = u_new
    half_out[...] = u_new.astype(jnp.bfloat16)


def rows(line, u, row_half, residues, halves, before=()):
    return line.call(
        functools.partial(rows_kernel, len(before)),
        "rows_step",
        (u, row_half, *before, *residues, *halves),
        [like(u), like(row_half)],
        aliases={0: 0, 1: 1},
    )


def last_kernel(tile, u_ref, row_half, dense, live, c_ref, acc, _, *refs):
    n = CHUNKS - 1
    done, (u_hbm, c_hbm, u_new, c_new, sems) = refs[:n], refs[n:]
    copies = []

    def copy(source, target, at):
        place = pl.ds(at, source.shape[0])
        copies.append(pltpu.make_async_copy(source, target.at[place], sems.at[len(copies)]))
        copies[-1].start()

    for h, c in enumerate(done):
        copy(c, c_hbm, chunk_span(h, c_hbm.shape[0]).start)
    at = chunk_span(n, c_hbm.shape[0])
    cols = c_ref[...]
    col_half = cols.astype(jnp.bfloat16)
    grad_cols = None
    for r in range(u_ref.shape[0] // tile):
        part = span(r, tile)
        half = row_half[part]
        residue = residue_of(at.start, tile, half, col_half, dense[at, part], live[:, part])
        grad = acc[part] + dot(residue, col_half, ((0,), (0,)))
        u_new[part] = sgd(u_ref[part], grad)
        copy(u_new.at[pl.ds(r * tile, tile)], u_hbm, r * tile)
        grad = dot(residue, half, ((1,), (0,)))
        grad_cols = grad if grad_cols is None else grad_cols + grad
    c_new[...] = sgd(cols, grad_cols)
    copy(c_new, c_hbm, at.start)
    for started in copies:
        started.wait()


def final(line, tile, u, row_half, cs, laid):
    n = CHUNKS - 1
    cols, rank = laid[0].shape[0], u.shape[1]
    steps = [columns(line, h, tile, row_half, cs[h], laid) for h in range(n)]
    done, residues, halves = zip(*steps)
    acc = gradient(line, u, residues, halves)
    return call(
        functools.partial(last_kernel, tile),
        "last_columns_and_rows",
        (u, row_half, *laid, cs[n], acc, line.turn, *done),
        [VMEM] * (7 + n),
        [like(u), like(u, (cols, rank))],
        [HBM, HBM],
        scratch=[
            pltpu.VMEM(u.shape, u.dtype),
            pltpu.VMEM(cs[n].shape, u.dtype),
            pltpu.SemaphoreType.DMA((CHUNKS + u.shape[0] // tile,)),
        ],
    )


def shifted(chunk, axis):
    n = lax.axis_size(axis)
    return lax.ppermute(chunk, axis, [(i, (i + 1) % n) for i in range(n)])


def per_device(row_factors, col_factors, tile_values, tile_coords, tile_counts):
    tile = tile_values.shape[2]
    strata = tile_values.shape[0]
    coords, counts = tile_coords.transpose(0, 2, 1), tile_counts.transpose(1, 0)
    sizes = row_factors.shape[0], col_factors.shape[0]
    u, c, row_half, *laid0, turn, done, residue, half = first(
        row_factors, col_factors, tile_values, coords, counts
    )
    line = Line(turn)
    cs = [shifted(done, "blk")]
    residues, halves, *done = others(line, tile, row_half, c, laid0)
    cs += [shifted(d, "blk") for d in done]
    laid = layout(line, tile_values, coords, counts, *sizes)
    u, row_half = rows(line, u, row_half, (residue, residues), (half, halves))

    for stratum in range(1, strata - 1):
        axis = "group" if stratum == 2 else "blk"
        arrived, cs, residues, halves, before = cs, [], [], [], ()
        for h in range(CHUNKS):
            done, residue, half = columns(line, h, tile, row_half, arrived[h], laid[stratum - 1])
            cs.append(shifted(done, axis))
            residues.append(residue)
            halves.append(half)
            if stratum == 1 and h == CHUNKS - 2:
                before = (gradient(line, u, residues, halves),)
                residues, halves = [], []
        u, row_half = rows(line, u, row_half, residues, halves, before)
    return final(line, tile, u, row_half, cs, laid[-1])


def solution(mesh):
    return jax.shard_map(
        per_device,
        mesh=mesh,
        in_specs=(
            P(("blk", "group"), None),
            P(("blk", "group"), None),
            P(None, ("blk", "group"), None, None),
            P(None, ("blk", "group"), None),
            P(None, ("blk", "group")),
        ),
        out_specs=(P(("blk", "group"), None), P(("blk", "group"), None)),
        check_vma=False,
    )
```

```python
import functools

import jax
import jax.numpy as jnp
from jax import lax
from jax.experimental import pallas as pl
from jax.experimental.pallas import tpu as pltpu
from jax.sharding import PartitionSpec as P

LEARN_RATE = 0.03
DECAY_RATE = 0.1
EDGES = (0, 3, 8, 13, 16)
CHUNKS = len(EDGES) - 1
WEIGHTS = (10**9, 10**7, 6 * 10**8, 2 * 10**9)
SUBLANES = 8

VMEM = pl.BlockSpec(memory_space=pltpu.VMEM)
SMEM = pl.BlockSpec(memory_space=pltpu.SMEM)
HBM = pl.BlockSpec(memory_space=pltpu.HBM)
ANY = pl.BlockSpec(memory_space=pl.ANY)


def call(body, name, operands, in_specs, outs, out_specs, flops=10**7, aliases=None, scratch=()):
    return pl.pallas_call(
        body,
        out_shape=outs,
        in_specs=in_specs,
        out_specs=out_specs,
        input_output_aliases=aliases or {},
        scratch_shapes=list(scratch),
        compiler_params=pltpu.CompilerParams(vmem_limit_bytes=24 * 1024 * 1024),
        cost_estimate=pl.CostEstimate(flops=flops, bytes_accessed=1, transcendentals=0),
        name=name,
    )(*operands)


class Line:
    def __init__(self, turn):
        self.turn = turn

    def call(self, body, name, operands, outs, flops=10**7, aliases=None):
        n_in = len(operands)

        def inner(*refs):
            body(*refs[:n_in], *refs[n_in + 2 :])

        self.turn, *out = call(
            inner,
            name,
            (*operands, self.turn),
            [VMEM] * (n_in + 1),
            [like(self.turn), *outs],
            [VMEM] * (1 + len(outs)),
            flops,
            {n_in: 0, **{i: o + 1 for i, o in (aliases or {}).items()}},
        )
        return out


def like(array, shape=None, dtype=None):
    return jax.ShapeDtypeStruct(shape or array.shape, dtype or array.dtype)


def span(h, width):
    return slice(h * width, (h + 1) * width)


def chunk_span(h, cols):
    return slice(cols * EDGES[h] // 16, cols * EDGES[h + 1] // 16)


def chunk_width(h, cols):
    at = chunk_span(h, cols)
    return at.stop - at.start


def scatter(stratum, values, coords, counts, dense, live):
    listed, tile, _ = values.shape
    col = lax.broadcasted_iota(jnp.int32, live.shape, 0)
    row = lax.broadcasted_iota(jnp.int32, live.shape, 1)
    named = jnp.zeros(live.shape, jnp.float32)
    for t in range(listed):
        r = pl.multiple_of(coords[stratum, 0, t] * tile, tile)
        c = coords[stratum, 1, t]
        dense[pl.ds(pl.multiple_of(c * tile, tile), tile), pl.ds(r, tile)] = values[t].T
        alive_c = jnp.where(t < counts[0, stratum], c, -1)
        named = jnp.where((col == alive_c) & (row >= r) & (row < r + tile), 1.0, named)
    live[...] = named


def sgd(old, grad):
    return old + LEARN_RATE * (grad - DECAY_RATE * old)


def dot(a, b, contract):
    return lax.dot_general(a, b, (contract, ((), ())), preferred_element_type=jnp.float32)


def columns_step(start, tile, row_half, cols, dense, live):
    col_half = cols.astype(jnp.bfloat16)
    estimate = dot(col_half, row_half, ((1,), (1,)))
    parts, at, stop = [], start, start + cols.shape[0]
    while at < stop:
        c = at // tile
        end = min((c + 1) * tile, stop)
        here = slice(at - start, end - start)
        residue = dense[here].astype(jnp.float32) - estimate[here]
        parts.append(jnp.where(live[c : c + 1] > 0, residue, 0.0).astype(jnp.bfloat16))
        at = end
    residue = parts[0] if len(parts) == 1 else jnp.concatenate(parts, axis=0)
    return residue, col_half, sgd(cols, dot(residue, row_half, ((1,), (0,))))


def rows_gradient(residues, halves):
    return sum(dot(e[...], c[...], ((0,), (0,))) for e, c in zip(residues, halves))


def first_kernel(u_hbm, c_hbm, x_hbm, coords_hbm, counts_hbm, *refs):
    u_ref, c_ref, half_ref, dense, live, turn, c_out, residue, col_half = refs[:9]
    x_ref, coords, counts, sems = refs[9:]
    width, tile = c_out.shape[0], x_ref.shape[1]
    cols = c_ref.shape[0]
    head, tail = pl.ds(0, width), pl.ds(width, cols - width)
    pairs = [(coords_hbm, coords), (counts_hbm, counts), (x_hbm.at[0], x_ref), (u_hbm, u_ref)]
    pairs += [(c_hbm.at[at], c_ref.at[at]) for at in (head, tail)]
    copies = [pltpu.make_async_copy(s, d, sems.at[i]) for i, (s, d) in enumerate(pairs)]
    for i in (3, 0, 1, 2, 4, 5):
        copies[i].start()
    turn[...] = jnp.zeros_like(turn)
    for copy in copies[:3]:
        copy.wait()
    scatter(0, x_ref, coords, counts, dense, live)
    copies[3].wait()
    row_half = u_ref[...].astype(jnp.bfloat16)
    half_ref[...] = row_half
    copies[4].wait()
    residue[...], col_half[...], c_out[...] = columns_step(
        0, tile, row_half, c_ref[:width], dense[:width], live
    )
    copies[5].wait()


def first(u, c, values, coords, counts):
    rows, cols = u.shape[0], c.shape[0]
    part = (chunk_width(0, cols), c.shape[1])
    bf16 = jnp.bfloat16
    outs = [like(u), like(c), like(u, dtype=bf16), like(u, (cols, rows), bf16)]
    outs += [like(u, (SUBLANES, rows)), like(u, (SUBLANES, 128))]
    outs += [like(c, part), like(u, (part[0], rows), bf16), like(c, part, bf16)]
    operands = (u, c, values, coords, counts)
    return call(
        first_kernel,
        "first_chunk",
        [pltpu.with_memory_space_constraint(x, pltpu.HBM) for x in operands],
        [HBM] * 5,
        outs,
        [VMEM] * len(outs),
        scratch=[
            pltpu.VMEM(values.shape[1:], values.dtype),
            pltpu.SMEM(coords.shape, coords.dtype),
            pltpu.SMEM(counts.shape, counts.dtype),
            pltpu.SemaphoreType.DMA((6,)),
        ],
    )


def other_kernel(tile, row_half, c_ref, dense, live, residue, col_half, *c_outs):
    start, cols = c_ref.shape[0] - residue.shape[0], c_ref.shape[0]
    rest = slice(start, cols)
    residue[...], col_half[...], new = columns_step(
        start, tile, row_half[...], c_ref[rest], dense[rest], live
    )
    for h, c_out in enumerate(c_outs, 1):
        at = chunk_span(h, cols)
        c_out[...] = new[at.start - start : at.stop - start]


def others(line, tile, row_half, c, laid):
    cols, rank = c.shape
    rest = cols - chunk_width(0, cols)
    outs = [like(row_half, (rest, row_half.shape[0])), like(row_half, (rest, rank))]
    return line.call(
        functools.partial(other_kernel, tile),
        "other_chunks",
        (row_half, c, *laid),
        outs + [like(c, (chunk_width(h, cols), rank)) for h in range(1, CHUNKS)],
    )


def layout_kernel(x_ref, coords, counts, *refs):
    outs = refs[2:]
    later = len(outs) // 2
    for s in range(later):
        scatter(s + 1, x_ref.at[s + 1], coords, counts, outs[s], outs[later + s])


def layout(line, values, coords, counts, rows, cols):
    later = values.shape[0] - 1
    outs = [like(values, (cols, rows))] * later
    outs += [like(values, (SUBLANES, rows), jnp.float32)] * later
    line.turn, *out = call(
        layout_kernel,
        "lay_out_tiles",
        (values, coords, counts, line.turn),
        [VMEM, SMEM, SMEM, VMEM],
        [like(line.turn), *outs],
        [VMEM] * (1 + len(outs)),
        aliases={3: 0},
    )
    return list(zip(out[:later], out[later:]))


def columns_kernel(h, tile, row_half, c_ref, dense, live, c_out, residue, col_half):
    at = chunk_span(h, dense.shape[0])
    residue[...], col_half[...], c_out[...] = columns_step(
        at.start, tile, row_half[...], c_ref[...], dense[at], live
    )


def columns(line, h, tile, row_half, c, laid):
    return line.call(
        functools.partial(columns_kernel, h, tile),
        "columns_step",
        (row_half, c, *laid),
        [like(c), like(row_half, (c.shape[0], row_half.shape[0])), like(c, dtype=jnp.bfloat16)],
        flops=WEIGHTS[h],
    )


def rows_kernel(_, __, *refs):
    *pairs, u_out, half_out = refs
    n = len(pairs) // 2
    u_new = sgd(u_out[...], rows_gradient(pairs[:n], pairs[n:]))
    u_out[...] = u_new
    half_out[...] = u_new.astype(jnp.bfloat16)


def rows(line, u, row_half, residues, halves):
    return line.call(
        rows_kernel,
        "rows_step",
        (u, row_half, *residues, *halves),
        [like(u), like(row_half)],
        aliases={0: 0, 1: 1},
    )


def gradient_kernel(*refs):
    *pairs, acc = refs
    n = len(pairs) // 2
    acc[...] = rows_gradient(pairs[:n], pairs[n:])


def last_kernel(tile, u_ref, row_half, dense, live, c_ref, acc, _, *refs):
    n = CHUNKS - 1
    done, (u_hbm, c_hbm, u_new, c_new, sems) = refs[:n], refs[n:]
    cols = c_hbm.shape[0]
    copies = []

    def copy(source, target, at):
        place = pl.ds(at, source.shape[0])
        copies.append(pltpu.make_async_copy(source, target.at[place], sems.at[len(copies)]))
        copies[-1].start()

    for h, c in enumerate(done):
        copy(c, c_hbm, chunk_span(h, cols).start)
    at = chunk_span(n, cols)
    residue, col_half, new_cols = columns_step(
        at.start, tile, row_half[...], c_ref[...], dense[at], live
    )
    for r in range(u_ref.shape[0] // tile):
        part = span(r, tile)
        grad = acc[part] + dot(residue[:, part], col_half, ((0,), (0,)))
        u_new[part] = sgd(u_ref[part], grad)
        copy(u_new.at[pl.ds(r * tile, tile)], u_hbm, r * tile)
    c_new[...] = new_cols
    copy(c_new, c_hbm, at.start)
    for started in copies:
        started.wait()


def final(line, tile, u, row_half, cs, laid):
    n = CHUNKS - 1
    cols, rank = laid[0].shape[0], u.shape[1]
    steps = [columns(line, h, tile, row_half, cs[h], laid) for h in range(n)]
    done, residues, halves = zip(*steps)
    (acc,) = line.call(
        gradient_kernel,
        "rows_gradient",
        (*residues, *halves),
        [like(u)],
    )
    return call(
        functools.partial(last_kernel, tile),
        "last_columns_and_rows",
        (u, row_half, *laid, cs[n], acc, line.turn, *done),
        [VMEM] * (7 + n),
        [like(u), like(u, (cols, rank))],
        [HBM, HBM],
        scratch=[
            pltpu.VMEM(u.shape, u.dtype),
            pltpu.VMEM(cs[n].shape, u.dtype),
            pltpu.SemaphoreType.DMA((CHUNKS + u.shape[0] // tile,)),
        ],
    )


def shifted(chunk, axis):
    n = lax.axis_size(axis)
    return lax.ppermute(chunk, axis, [(i, (i + 1) % n) for i in range(n)])


def per_device(row_factors, col_factors, tile_values, tile_coords, tile_counts):
    tile = tile_values.shape[2]
    strata = tile_values.shape[0]
    coords, counts = tile_coords.transpose(0, 2, 1), tile_counts.transpose(1, 0)
    sizes = row_factors.shape[0], col_factors.shape[0]
    u, c, row_half, *laid0, turn, done, residue, half = first(
        row_factors, col_factors, tile_values, coords, counts
    )
    line = Line(turn)
    cs = [shifted(done, "blk")]
    residues, halves, *done = others(line, tile, row_half, c, laid0)
    cs += [shifted(d, "blk") for d in done]
    laid = layout(line, tile_values, coords, counts, *sizes)
    u, row_half = rows(line, u, row_half, (residue, residues), (half, halves))

    for stratum in range(1, strata - 1):
        axis = "group" if stratum == 2 else "blk"
        arrived, cs, residues, halves = cs, [], [], []
        for h in range(CHUNKS):
            done, residue, half = columns(line, h, tile, row_half, arrived[h], laid[stratum - 1])
            cs.append(shifted(done, axis))
            residues.append(residue)
            halves.append(half)
        u, row_half = rows(line, u, row_half, residues, halves)
    return final(line, tile, u, row_half, cs, laid[-1])


def solution(mesh):
    return jax.shard_map(
        per_device,
        mesh=mesh,
        in_specs=(
            P(("blk", "group"), None),
            P(("blk", "group"), None),
            P(None, ("blk", "group"), None, None),
            P(None, ("blk", "group"), None),
            P(None, ("blk", "group")),
        ),
        out_specs=(P(("blk", "group"), None), P(("blk", "group"), None)),
        check_vma=False,
    )
```

```python
import functools

import jax
import jax.numpy as jnp
from jax import lax
from jax.experimental import pallas as pl
from jax.experimental.pallas import tpu as pltpu
from jax.sharding import PartitionSpec as P

LEARN_RATE = 0.03
DECAY_RATE = 0.1
EARLY = (0, 3, 8, 13, 16)
LATER = (0, 3, 8, 11, 14, 16)
EARLY_WEIGHTS = (1e9, 1e7, 6e8, 2e9)
LATER_WEIGHTS = (3e8, 1e8, 3e8, 6e8, 6e8)
SUBLANES = 8

VMEM = pl.BlockSpec(memory_space=pltpu.VMEM)
SMEM = pl.BlockSpec(memory_space=pltpu.SMEM)
HBM = pl.BlockSpec(memory_space=pltpu.HBM)
ANY = pl.BlockSpec(memory_space=pl.ANY)


def call(body, name, operands, in_specs, outs, out_specs, flops=10**7, aliases=None, scratch=()):
    return pl.pallas_call(
        body,
        out_shape=outs,
        in_specs=in_specs,
        out_specs=out_specs,
        input_output_aliases=aliases or {},
        scratch_shapes=list(scratch),
        compiler_params=pltpu.CompilerParams(vmem_limit_bytes=24 * 1024 * 1024),
        cost_estimate=pl.CostEstimate(flops=flops, bytes_accessed=1, transcendentals=0),
        name=name,
    )(*operands)


class Line:
    def __init__(self, turn):
        self.turn = turn

    def call(self, body, name, operands, outs, flops=10**7, aliases=None):
        n_in = len(operands)

        def inner(*refs):
            body(*refs[:n_in], *refs[n_in + 2 :])

        self.turn, *out = call(
            inner,
            name,
            (*operands, self.turn),
            [VMEM] * (n_in + 1),
            [like(self.turn), *outs],
            [VMEM] * (1 + len(outs)),
            flops,
            {n_in: 0, **{i: o + 1 for i, o in (aliases or {}).items()}},
        )
        return out


def like(array, shape=None, dtype=None):
    return jax.ShapeDtypeStruct(shape or array.shape, dtype or array.dtype)


def span(h, width):
    return slice(h * width, (h + 1) * width)


def spans(edges, cols):
    return [slice(cols * i // 16, cols * j // 16) for i, j in zip(edges, edges[1:])]


def size(at):
    return at.stop - at.start


def scatter(stratum, values, coords, counts, dense, live):
    listed, tile, _ = values.shape
    col = lax.broadcasted_iota(jnp.int32, live.shape, 0)
    row = lax.broadcasted_iota(jnp.int32, live.shape, 1)
    named = jnp.zeros(live.shape, jnp.float32)
    for t in range(listed):
        r = pl.multiple_of(coords[stratum, 0, t] * tile, tile)
        c = coords[stratum, 1, t]
        dense[pl.ds(pl.multiple_of(c * tile, tile), tile), pl.ds(r, tile)] = values[t].T
        alive_c = jnp.where(t < counts[0, stratum], c, -1)
        named = jnp.where((col == alive_c) & (row >= r) & (row < r + tile), 1.0, named)
    live[...] = named


def sgd(old, grad):
    return old + LEARN_RATE * (grad - DECAY_RATE * old)


def dot(a, b, contract):
    return lax.dot_general(a, b, (contract, ((), ())), preferred_element_type=jnp.float32)


def columns_step(start, tile, row_half, cols, dense, live):
    col_half = cols.astype(jnp.bfloat16)
    estimate = dot(col_half, row_half, ((1,), (1,)))
    parts, at, stop = [], start, start + cols.shape[0]
    while at < stop:
        c = at // tile
        end = min((c + 1) * tile, stop)
        here = slice(at - start, end - start)
        residue = dense[here].astype(jnp.float32) - estimate[here]
        parts.append(jnp.where(live[c : c + 1] > 0, residue, 0.0).astype(jnp.bfloat16))
        at = end
    residue = parts[0] if len(parts) == 1 else jnp.concatenate(parts, axis=0)
    return residue, col_half, sgd(cols, dot(residue, row_half, ((1,), (0,))))


def rows_gradient(residues, halves):
    return sum(dot(e[...], c[...], ((0,), (0,))) for e, c in zip(residues, halves))


def first_kernel(u_hbm, c_hbm, x_hbm, coords_hbm, counts_hbm, *refs):
    u_ref, c_ref, half_ref, dense, live, turn, c_out, residue, col_half = refs[:9]
    x_ref, coords, counts, sems = refs[9:]
    width, tile = c_out.shape[0], x_ref.shape[1]
    cols = c_ref.shape[0]
    head, tail = pl.ds(0, width), pl.ds(width, cols - width)
    pairs = [(coords_hbm, coords), (counts_hbm, counts), (x_hbm.at[0], x_ref), (u_hbm, u_ref)]
    pairs += [(c_hbm.at[at], c_ref.at[at]) for at in (head, tail)]
    copies = [pltpu.make_async_copy(s, d, sems.at[i]) for i, (s, d) in enumerate(pairs)]
    for copy in copies:
        copy.start()
    turn[...] = jnp.zeros_like(turn)
    for copy in copies[:3]:
        copy.wait()
    scatter(0, x_ref, coords, counts, dense, live)
    copies[3].wait()
    row_half = u_ref[...].astype(jnp.bfloat16)
    half_ref[...] = row_half
    copies[4].wait()
    residue[...], col_half[...], c_out[...] = columns_step(
        0, tile, row_half, c_ref[:width], dense[:width], live
    )
    copies[5].wait()


def first(u, c, values, coords, counts):
    rows, cols = u.shape[0], c.shape[0]
    part = (size(spans(EARLY, cols)[0]), c.shape[1])
    bf16 = jnp.bfloat16
    outs = [like(u), like(c), like(u, dtype=bf16), like(u, (cols, rows), bf16)]
    outs += [like(u, (SUBLANES, rows)), like(u, (SUBLANES, 128))]
    outs += [like(c, part), like(u, (part[0], rows), bf16), like(c, part, bf16)]
    operands = (u, c, values, coords, counts)
    return call(
        first_kernel,
        "first_chunk",
        [pltpu.with_memory_space_constraint(x, pltpu.HBM) for x in operands],
        [HBM] * 5,
        outs,
        [VMEM] * len(outs),
        scratch=[
            pltpu.VMEM(values.shape[1:], values.dtype),
            pltpu.SMEM(coords.shape, coords.dtype),
            pltpu.SMEM(counts.shape, counts.dtype),
            pltpu.SemaphoreType.DMA((6,)),
        ],
    )


def other_kernel(tile, row_half, c_ref, dense, live, residue, col_half, *c_outs):
    start, cols = c_ref.shape[0] - residue.shape[0], c_ref.shape[0]
    rest = slice(start, cols)
    residue[...], col_half[...], new = columns_step(
        start, tile, row_half[...], c_ref[rest], dense[rest], live
    )
    for at, c_out in zip(spans(EARLY, cols)[1:], c_outs):
        c_out[...] = new[at.start - start : at.stop - start]


def others(line, tile, row_half, c, laid):
    cols, rank = c.shape
    chunks = spans(EARLY, cols)[1:]
    rest = cols - chunks[0].start
    outs = [like(row_half, (rest, row_half.shape[0])), like(row_half, (rest, rank))]
    return line.call(
        functools.partial(other_kernel, tile),
        "other_chunks",
        (row_half, c, *laid),
        outs + [like(c, (size(at), rank)) for at in chunks],
    )


def layout_kernel(x_ref, coords, counts, *refs):
    outs = refs[2:]
    later = len(outs) // 2
    for s in range(later):
        scatter(s + 1, x_ref.at[s + 1], coords, counts, outs[s], outs[later + s])


def layout(line, values, coords, counts, rows, cols):
    later = values.shape[0] - 1
    outs = [like(values, (cols, rows))] * later
    outs += [like(values, (SUBLANES, rows), jnp.float32)] * later
    line.turn, *out = call(
        layout_kernel,
        "lay_out_tiles",
        (values, coords, counts, line.turn),
        [VMEM, SMEM, SMEM, VMEM],
        [like(line.turn), *outs],
        [VMEM] * (1 + len(outs)),
        aliases={3: 0},
    )
    return list(zip(out[:later], out[later:]))


def columns_kernel(at, cuts, tile, row_half, dense, live, *refs):
    *cs, c_out, residue, col_half = refs
    parts = [c[cut] for c, cut in zip(cs, cuts)]
    cols = parts[0] if len(parts) == 1 else jnp.concatenate(parts, axis=0)
    residue[...], col_half[...], c_out[...] = columns_step(
        at.start, tile, row_half[...], cols, dense[at], live
    )


def columns(line, at, weight, tile, row_half, arrived, laid):
    cs, cuts = [], []
    for there, c in arrived:
        start, stop = max(at.start, there.start), min(at.stop, there.stop)
        if start < stop:
            cs.append(c)
            cuts.append(slice(start - there.start, stop - there.start))
    rows, rank = row_half.shape
    part, bf16 = (size(at), rank), jnp.bfloat16
    return line.call(
        functools.partial(columns_kernel, at, cuts, tile),
        "columns_step",
        (row_half, *laid, *cs),
        [like(cs[0], part), like(row_half, (size(at), rows)), like(row_half, part, bf16)],
        flops=int(weight),
    )


def rows_kernel(_, __, *refs):
    *pairs, u_out, half_out = refs
    n = len(pairs) // 2
    u_new = sgd(u_out[...], rows_gradient(pairs[:n], pairs[n:]))
    u_out[...] = u_new
    half_out[...] = u_new.astype(jnp.bfloat16)


def rows(line, u, row_half, residues, halves):
    return line.call(
        rows_kernel,
        "rows_step",
        (u, row_half, *residues, *halves),
        [like(u), like(row_half)],
        aliases={0: 0, 1: 1},
    )


def gradient_kernel(*refs):
    *pairs, acc = refs
    n = len(pairs) // 2
    acc[...] = rows_gradient(pairs[:n], pairs[n:])


def last_kernel(tile, u_ref, row_half, dense, live, c_ref, acc, _, *refs):
    n = len(LATER) - 2
    done, (u_hbm, c_hbm, u_new, c_new, sems) = refs[:n], refs[n:]
    chunks = spans(LATER, c_hbm.shape[0])
    copies = []

    def copy(source, target, at):
        place = pl.ds(at, source.shape[0])
        copies.append(pltpu.make_async_copy(source, target.at[place], sems.at[len(copies)]))
        copies[-1].start()

    for h, c in enumerate(done):
        copy(c, c_hbm, chunks[h].start)
    at = chunks[n]
    residue, col_half, new_cols = columns_step(
        at.start, tile, row_half[...], c_ref[...], dense[at], live
    )
    for r in range(u_ref.shape[0] // tile):
        part = span(r, tile)
        grad = acc[part] + dot(residue[:, part], col_half, ((0,), (0,)))
        u_new[part] = sgd(u_ref[part], grad)
        copy(u_new.at[pl.ds(r * tile, tile)], u_hbm, r * tile)
    c_new[...] = new_cols
    copy(c_new, c_hbm, at.start)
    for started in copies:
        started.wait()


def final(line, tile, u, row_half, cs, laid):
    cols, rank = laid[0].shape[0], u.shape[1]
    *before, _ = spans(LATER, cols)
    n = len(before)
    steps = [
        columns(line, at, weight, tile, row_half, cs[h : h + 1], laid)
        for h, (at, weight) in enumerate(zip(before, LATER_WEIGHTS))
    ]
    done, residues, halves = zip(*steps)
    (acc,) = line.call(
        gradient_kernel,
        "rows_gradient",
        (*residues, *halves),
        [like(u)],
    )
    return call(
        functools.partial(last_kernel, tile),
        "last_columns_and_rows",
        (u, row_half, *laid, cs[n][1], acc, line.turn, *done),
        [VMEM] * (7 + n),
        [like(u), like(u, (cols, rank))],
        [HBM, HBM],
        scratch=[
            pltpu.VMEM(u.shape, u.dtype),
            pltpu.VMEM(cs[n][1].shape, u.dtype),
            pltpu.SemaphoreType.DMA((n + 1 + u.shape[0] // tile,)),
        ],
    )


def shifted(chunk, axis):
    n = lax.axis_size(axis)
    return lax.ppermute(chunk, axis, [(i, (i + 1) % n) for i in range(n)])


def per_device(row_factors, col_factors, tile_values, tile_coords, tile_counts):
    tile = tile_values.shape[2]
    strata = tile_values.shape[0]
    coords, counts = tile_coords.transpose(0, 2, 1), tile_counts.transpose(1, 0)
    sizes = row_factors.shape[0], col_factors.shape[0]
    u, c, row_half, *laid0, turn, done, residue, half = first(
        row_factors, col_factors, tile_values, coords, counts
    )
    line = Line(turn)
    cs = [shifted(done, "blk")]
    residues, halves, *done = others(line, tile, row_half, c, laid0)
    cs += [shifted(d, "blk") for d in done]
    laid = layout(line, tile_values, coords, counts, *sizes)
    u, row_half = rows(line, u, row_half, (residue, residues), (half, halves))

    cs = list(zip(spans(EARLY, sizes[1]), cs))
    for stratum in range(1, strata - 1):
        axis = "group" if stratum == 2 else "blk"
        edges, weights = (EARLY, EARLY_WEIGHTS) if stratum < 2 else (LATER, LATER_WEIGHTS)
        arrived, cs, residues, halves = cs, [], [], []
        for at, weight in zip(spans(edges, sizes[1]), weights):
            done, residue, half = columns(
                line, at, weight, tile, row_half, arrived, laid[stratum - 1]
            )
            cs.append((at, shifted(done, axis)))
            residues.append(residue)
            halves.append(half)
        u, row_half = rows(line, u, row_half, residues, halves)
    return final(line, tile, u, row_half, cs, laid[-1])


def solution(mesh):
    return jax.shard_map(
        per_device,
        mesh=mesh,
        in_specs=(
            P(("blk", "group"), None),
            P(("blk", "group"), None),
            P(None, ("blk", "group"), None, None),
            P(None, ("blk", "group"), None),
            P(None, ("blk", "group")),
        ),
        out_specs=(P(("blk", "group"), None), P(("blk", "group"), None)),
        check_vma=False,
    )
```

```python
import functools

import jax
import jax.numpy as jnp
from jax import lax
from jax.experimental import pallas as pl
from jax.experimental.pallas import tpu as pltpu
from jax.sharding import PartitionSpec as P

LEARN_RATE = 0.03
DECAY_RATE = 0.1
EARLY = (0, 3, 8, 13, 16)
LATER = (0, 3, 6, 11, 14, 16)
EARLY_WEIGHTS = (1e9, 1e7, 6e8, 2e9)
LATER_WEIGHTS = (3e8, 1e8, 3e8, 6e8, 6e8)
SUBLANES = 8

VMEM = pl.BlockSpec(memory_space=pltpu.VMEM)
SMEM = pl.BlockSpec(memory_space=pltpu.SMEM)
HBM = pl.BlockSpec(memory_space=pltpu.HBM)
ANY = pl.BlockSpec(memory_space=pl.ANY)


def call(body, name, operands, in_specs, outs, out_specs, flops=10**7, aliases=None, scratch=()):
    return pl.pallas_call(
        body,
        out_shape=outs,
        in_specs=in_specs,
        out_specs=out_specs,
        input_output_aliases=aliases or {},
        scratch_shapes=list(scratch),
        compiler_params=pltpu.CompilerParams(vmem_limit_bytes=24 * 1024 * 1024),
        cost_estimate=pl.CostEstimate(flops=flops, bytes_accessed=1, transcendentals=0),
        name=name,
    )(*operands)


class Line:
    def __init__(self, turn):
        self.turn = turn

    def call(self, body, name, operands, outs, flops=10**7, aliases=None):
        n_in = len(operands)

        def inner(*refs):
            body(*refs[:n_in], *refs[n_in + 2 :])

        self.turn, *out = call(
            inner,
            name,
            (*operands, self.turn),
            [VMEM] * (n_in + 1),
            [like(self.turn), *outs],
            [VMEM] * (1 + len(outs)),
            flops,
            {n_in: 0, **{i: o + 1 for i, o in (aliases or {}).items()}},
        )
        return out


def like(array, shape=None, dtype=None):
    return jax.ShapeDtypeStruct(shape or array.shape, dtype or array.dtype)


def span(h, width):
    return slice(h * width, (h + 1) * width)


def spans(edges, cols):
    return [slice(cols * i // 16, cols * j // 16) for i, j in zip(edges, edges[1:])]


def size(at):
    return at.stop - at.start


def scatter(stratum, values, coords, counts, dense, live):
    listed, tile, _ = values.shape
    col = lax.broadcasted_iota(jnp.int32, live.shape, 0)
    row = lax.broadcasted_iota(jnp.int32, live.shape, 1)
    named = jnp.zeros(live.shape, jnp.float32)
    for t in range(listed):
        r = pl.multiple_of(coords[stratum, 0, t] * tile, tile)
        c = coords[stratum, 1, t]
        dense[pl.ds(pl.multiple_of(c * tile, tile), tile), pl.ds(r, tile)] = values[t].T
        alive_c = jnp.where(t < counts[0, stratum], c, -1)
        named = jnp.where((col == alive_c) & (row >= r) & (row < r + tile), 1.0, named)
    live[...] = named


def sgd(old, grad):
    return old + LEARN_RATE * (grad - DECAY_RATE * old)


def dot(a, b, contract):
    return lax.dot_general(a, b, (contract, ((), ())), preferred_element_type=jnp.float32)


def columns_step(start, tile, row_half, cols, dense, live):
    col_half = cols.astype(jnp.bfloat16)
    estimate = dot(col_half, row_half, ((1,), (1,)))
    parts, at, stop = [], start, start + cols.shape[0]
    while at < stop:
        c = at // tile
        end = min((c + 1) * tile, stop)
        here = slice(at - start, end - start)
        residue = dense[here].astype(jnp.float32) - estimate[here]
        parts.append(jnp.where(live[c : c + 1] > 0, residue, 0.0).astype(jnp.bfloat16))
        at = end
    residue = parts[0] if len(parts) == 1 else jnp.concatenate(parts, axis=0)
    return residue, col_half, sgd(cols, dot(residue, row_half, ((1,), (0,))))


def rows_gradient(residues, halves):
    return sum(dot(e[...], c[...], ((0,), (0,))) for e, c in zip(residues, halves))


def first_kernel(u_hbm, c_hbm, x_hbm, coords_hbm, counts_hbm, *refs):
    u_ref, c_ref, half_ref, dense, live, turn, c_out, residue, col_half = refs[:9]
    x_ref, coords, counts, sems = refs[9:]
    width, tile = c_out.shape[0], x_ref.shape[1]
    cols = c_ref.shape[0]
    head, tail = pl.ds(0, width), pl.ds(width, cols - width)
    pairs = [(coords_hbm, coords), (counts_hbm, counts), (x_hbm.at[0], x_ref), (u_hbm, u_ref)]
    pairs += [(c_hbm.at[at], c_ref.at[at]) for at in (head, tail)]
    copies = [pltpu.make_async_copy(s, d, sems.at[i]) for i, (s, d) in enumerate(pairs)]
    for copy in copies:
        copy.start()
    turn[...] = jnp.zeros_like(turn)
    for copy in copies[:3]:
        copy.wait()
    scatter(0, x_ref, coords, counts, dense, live)
    copies[3].wait()
    row_half = u_ref[...].astype(jnp.bfloat16)
    half_ref[...] = row_half
    copies[4].wait()
    residue[...], col_half[...], c_out[...] = columns_step(
        0, tile, row_half, c_ref[:width], dense[:width], live
    )
    copies[5].wait()


def first(u, c, values, coords, counts):
    rows, cols = u.shape[0], c.shape[0]
    part = (size(spans(EARLY, cols)[0]), c.shape[1])
    bf16 = jnp.bfloat16
    outs = [like(u), like(c), like(u, dtype=bf16), like(u, (cols, rows), bf16)]
    outs += [like(u, (SUBLANES, rows)), like(u, (SUBLANES, 128))]
    outs += [like(c, part), like(u, (part[0], rows), bf16), like(c, part, bf16)]
    operands = (u, c, values, coords, counts)
    return call(
        first_kernel,
        "first_chunk",
        [pltpu.with_memory_space_constraint(x, pltpu.HBM) for x in operands],
        [HBM] * 5,
        outs,
        [VMEM] * len(outs),
        scratch=[
            pltpu.VMEM(values.shape[1:], values.dtype),
            pltpu.SMEM(coords.shape, coords.dtype),
            pltpu.SMEM(counts.shape, counts.dtype),
            pltpu.SemaphoreType.DMA((6,)),
        ],
    )


def other_kernel(tile, row_half, c_ref, dense, live, residue, col_half, *c_outs):
    start, cols = c_ref.shape[0] - residue.shape[0], c_ref.shape[0]
    rest = slice(start, cols)
    residue[...], col_half[...], new = columns_step(
        start, tile, row_half[...], c_ref[rest], dense[rest], live
    )
    for at, c_out in zip(spans(EARLY, cols)[1:], c_outs):
        c_out[...] = new[at.start - start : at.stop - start]


def others(line, tile, row_half, c, laid):
    cols, rank = c.shape
    chunks = spans(EARLY, cols)[1:]
    rest = cols - chunks[0].start
    outs = [like(row_half, (rest, row_half.shape[0])), like(row_half, (rest, rank))]
    return line.call(
        functools.partial(other_kernel, tile),
        "other_chunks",
        (row_half, c, *laid),
        outs + [like(c, (size(at), rank)) for at in chunks],
    )


def layout_kernel(x_ref, coords, counts, *refs):
    outs = refs[2:]
    later = len(outs) // 2
    for s in range(later):
        scatter(s + 1, x_ref.at[s + 1], coords, counts, outs[s], outs[later + s])


def layout(line, values, coords, counts, rows, cols):
    later = values.shape[0] - 1
    outs = [like(values, (cols, rows))] * later
    outs += [like(values, (SUBLANES, rows), jnp.float32)] * later
    line.turn, *out = call(
        layout_kernel,
        "lay_out_tiles",
        (values, coords, counts, line.turn),
        [VMEM, SMEM, SMEM, VMEM],
        [like(line.turn), *outs],
        [VMEM] * (1 + len(outs)),
        aliases={3: 0},
    )
    return list(zip(out[:later], out[later:]))


def columns_kernel(at, cuts, tile, row_half, dense, live, *refs):
    *cs, c_out, residue, col_half = refs
    parts = [c[cut] for c, cut in zip(cs, cuts)]
    cols = parts[0] if len(parts) == 1 else jnp.concatenate(parts, axis=0)
    residue[...], col_half[...], c_out[...] = columns_step(
        at.start, tile, row_half[...], cols, dense[at], live
    )


def columns(line, at, weight, tile, row_half, arrived, laid):
    cs, cuts = [], []
    for there, c in arrived:
        start, stop = max(at.start, there.start), min(at.stop, there.stop)
        if start < stop:
            cs.append(c)
            cuts.append(slice(start - there.start, stop - there.start))
    rows, rank = row_half.shape
    part, bf16 = (size(at), rank), jnp.bfloat16
    return line.call(
        functools.partial(columns_kernel, at, cuts, tile),
        "columns_step",
        (row_half, *laid, *cs),
        [like(cs[0], part), like(row_half, (size(at), rows)), like(row_half, part, bf16)],
        flops=int(weight),
    )


def rows_kernel(_, __, *refs):
    *pairs, u_out, half_out = refs
    n = len(pairs) // 2
    u_new = sgd(u_out[...], rows_gradient(pairs[:n], pairs[n:]))
    u_out[...] = u_new
    half_out[...] = u_new.astype(jnp.bfloat16)


def rows(line, u, row_half, residues, halves):
    return line.call(
        rows_kernel,
        "rows_step",
        (u, row_half, *residues, *halves),
        [like(u), like(row_half)],
        aliases={0: 0, 1: 1},
    )


def gradient_kernel(*refs):
    *pairs, acc = refs
    n = len(pairs) // 2
    acc[...] = rows_gradient(pairs[:n], pairs[n:])


def last_kernel(tile, u_ref, row_half, dense, live, c_ref, acc, _, *refs):
    n = len(LATER) - 2
    done, (u_hbm, c_hbm, u_new, c_new, sems) = refs[:n], refs[n:]
    chunks = spans(LATER, c_hbm.shape[0])
    copies = []

    def copy(source, target, at):
        place = pl.ds(at, source.shape[0])
        copies.append(pltpu.make_async_copy(source, target.at[place], sems.at[len(copies)]))
        copies[-1].start()

    for h, c in enumerate(done):
        copy(c, c_hbm, chunks[h].start)
    at = chunks[n]
    residue, col_half, new_cols = columns_step(
        at.start, tile, row_half[...], c_ref[...], dense[at], live
    )
    for r in range(u_ref.shape[0] // tile):
        part = span(r, tile)
        grad = acc[part] + dot(residue[:, part], col_half, ((0,), (0,)))
        u_new[part] = sgd(u_ref[part], grad)
        copy(u_new.at[pl.ds(r * tile, tile)], u_hbm, r * tile)
    c_new[...] = new_cols
    copy(c_new, c_hbm, at.start)
    for started in copies:
        started.wait()


def final(line, tile, u, row_half, cs, laid):
    cols, rank = laid[0].shape[0], u.shape[1]
    *before, _ = spans(LATER, cols)
    n = len(before)
    steps = [
        columns(line, at, weight, tile, row_half, cs[h : h + 1], laid)
        for h, (at, weight) in enumerate(zip(before, LATER_WEIGHTS))
    ]
    done, residues, halves = zip(*steps)
    (acc,) = line.call(
        gradient_kernel,
        "rows_gradient",
        (*residues, *halves),
        [like(u)],
    )
    return call(
        functools.partial(last_kernel, tile),
        "last_columns_and_rows",
        (u, row_half, *laid, cs[n][1], acc, line.turn, *done),
        [VMEM] * (7 + n),
        [like(u), like(u, (cols, rank))],
        [HBM, HBM],
        scratch=[
            pltpu.VMEM(u.shape, u.dtype),
            pltpu.VMEM(cs[n][1].shape, u.dtype),
            pltpu.SemaphoreType.DMA((n + 1 + u.shape[0] // tile,)),
        ],
    )


def shifted(chunk, axis):
    n = lax.axis_size(axis)
    return lax.ppermute(chunk, axis, [(i, (i + 1) % n) for i in range(n)])


def per_device(row_factors, col_factors, tile_values, tile_coords, tile_counts):
    tile = tile_values.shape[2]
    strata = tile_values.shape[0]
    coords, counts = tile_coords.transpose(0, 2, 1), tile_counts.transpose(1, 0)
    sizes = row_factors.shape[0], col_factors.shape[0]
    u, c, row_half, *laid0, turn, done, residue, half = first(
        row_factors, col_factors, tile_values, coords, counts
    )
    line = Line(turn)
    cs = [shifted(done, "blk")]
    residues, halves, *done = others(line, tile, row_half, c, laid0)
    cs += [shifted(d, "blk") for d in done]
    laid = layout(line, tile_values, coords, counts, *sizes)
    u, row_half = rows(line, u, row_half, (residue, residues), (half, halves))

    cs = list(zip(spans(EARLY, sizes[1]), cs))
    for stratum in range(1, strata - 1):
        axis = "group" if stratum == 2 else "blk"
        edges, weights = (EARLY, EARLY_WEIGHTS) if stratum < 2 else (LATER, LATER_WEIGHTS)
        arrived, cs, residues, halves = cs, [], [], []
        for at, weight in zip(spans(edges, sizes[1]), weights):
            done, residue, half = columns(
                line, at, weight, tile, row_half, arrived, laid[stratum - 1]
            )
            cs.append((at, shifted(done, axis)))
            residues.append(residue)
            halves.append(half)
        u, row_half = rows(line, u, row_half, residues, halves)
    return final(line, tile, u, row_half, cs, laid[-1])


def solution(mesh):
    return jax.shard_map(
        per_device,
        mesh=mesh,
        in_specs=(
            P(("blk", "group"), None),
            P(("blk", "group"), None),
            P(None, ("blk", "group"), None, None),
            P(None, ("blk", "group"), None),
            P(None, ("blk", "group")),
        ),
        out_specs=(P(("blk", "group"), None), P(("blk", "group"), None)),
        check_vma=False,
    )
```

```python
import functools

import jax
import jax.numpy as jnp
from jax import lax
from jax.experimental import pallas as pl
from jax.experimental.pallas import tpu as pltpu
from jax.sharding import PartitionSpec as P

LEARN_RATE = 0.03
DECAY_RATE = 0.1
EARLY = (0, 3, 8, 13, 16)
LATER = (0, 3, 7, 11, 14, 16)
EARLY_WEIGHTS = (1e9, 1e7, 6e8, 2e9)
LATER_WEIGHTS = (3e8, 1e8, 3e8, 6e8, 6e8)
SUBLANES = 8

VMEM = pl.BlockSpec(memory_space=pltpu.VMEM)
SMEM = pl.BlockSpec(memory_space=pltpu.SMEM)
HBM = pl.BlockSpec(memory_space=pltpu.HBM)
ANY = pl.BlockSpec(memory_space=pl.ANY)


def call(body, name, operands, in_specs, outs, out_specs, flops=10**7, aliases=None, scratch=()):
    return pl.pallas_call(
        body,
        out_shape=outs,
        in_specs=in_specs,
        out_specs=out_specs,
        input_output_aliases=aliases or {},
        scratch_shapes=list(scratch),
        compiler_params=pltpu.CompilerParams(vmem_limit_bytes=24 * 1024 * 1024),
        cost_estimate=pl.CostEstimate(flops=flops, bytes_accessed=1, transcendentals=0),
        name=name,
    )(*operands)


class Line:
    def __init__(self, turn):
        self.turn = turn

    def call(self, body, name, operands, outs, flops=10**7, aliases=None):
        n_in = len(operands)

        def inner(*refs):
            body(*refs[:n_in], *refs[n_in + 2 :])

        self.turn, *out = call(
            inner,
            name,
            (*operands, self.turn),
            [VMEM] * (n_in + 1),
            [like(self.turn), *outs],
            [VMEM] * (1 + len(outs)),
            flops,
            {n_in: 0, **{i: o + 1 for i, o in (aliases or {}).items()}},
        )
        return out


def like(array, shape=None, dtype=None):
    return jax.ShapeDtypeStruct(shape or array.shape, dtype or array.dtype)


def span(h, width):
    return slice(h * width, (h + 1) * width)


def spans(edges, cols):
    return [slice(cols * i // 16, cols * j // 16) for i, j in zip(edges, edges[1:])]


def size(at):
    return at.stop - at.start


def scatter(stratum, values, coords, counts, dense, live):
    listed, tile, _ = values.shape
    col = lax.broadcasted_iota(jnp.int32, live.shape, 0)
    row = lax.broadcasted_iota(jnp.int32, live.shape, 1)
    named = jnp.zeros(live.shape, jnp.float32)
    for t in range(listed):
        r = pl.multiple_of(coords[stratum, 0, t] * tile, tile)
        c = coords[stratum, 1, t]
        dense[pl.ds(pl.multiple_of(c * tile, tile), tile), pl.ds(r, tile)] = values[t].T
        alive_c = jnp.where(t < counts[0, stratum], c, -1)
        named = jnp.where((col == alive_c) & (row >= r) & (row < r + tile), 1.0, named)
    live[...] = named


def sgd(old, grad):
    return old + LEARN_RATE * (grad - DECAY_RATE * old)


def dot(a, b, contract):
    return lax.dot_general(a, b, (contract, ((), ())), preferred_element_type=jnp.float32)


def columns_step(start, tile, row_half, cols, dense, live):
    col_half = cols.astype(jnp.bfloat16)
    estimate = dot(col_half, row_half, ((1,), (1,)))
    parts, at, stop = [], start, start + cols.shape[0]
    while at < stop:
        c = at // tile
        end = min((c + 1) * tile, stop)
        here = slice(at - start, end - start)
        residue = dense[here].astype(jnp.float32) - estimate[here]
        parts.append(jnp.where(live[c : c + 1] > 0, residue, 0.0).astype(jnp.bfloat16))
        at = end
    residue = parts[0] if len(parts) == 1 else jnp.concatenate(parts, axis=0)
    return residue, col_half, sgd(cols, dot(residue, row_half, ((1,), (0,))))


def rows_gradient(residues, halves):
    return sum(dot(e[...], c[...], ((0,), (0,))) for e, c in zip(residues, halves))


def first_kernel(u_hbm, c_hbm, x_hbm, coords_hbm, counts_hbm, *refs):
    u_ref, c_ref, half_ref, dense, live, turn, c_out, residue, col_half = refs[:9]
    x_ref, coords, counts, sems = refs[9:]
    width, tile = c_out.shape[0], x_ref.shape[1]
    cols = c_ref.shape[0]
    head, tail = pl.ds(0, width), pl.ds(width, cols - width)
    pairs = [(coords_hbm, coords), (counts_hbm, counts), (x_hbm.at[0], x_ref), (u_hbm, u_ref)]
    pairs += [(c_hbm.at[at], c_ref.at[at]) for at in (head, tail)]
    copies = [pltpu.make_async_copy(s, d, sems.at[i]) for i, (s, d) in enumerate(pairs)]
    for copy in copies:
        copy.start()
    turn[...] = jnp.zeros_like(turn)
    for copy in copies[:3]:
        copy.wait()
    scatter(0, x_ref, coords, counts, dense, live)
    copies[3].wait()
    row_half = u_ref[...].astype(jnp.bfloat16)
    half_ref[...] = row_half
    copies[4].wait()
    residue[...], col_half[...], c_out[...] = columns_step(
        0, tile, row_half, c_ref[:width], dense[:width], live
    )
    copies[5].wait()


def first(u, c, values, coords, counts):
    rows, cols = u.shape[0], c.shape[0]
    part = (size(spans(EARLY, cols)[0]), c.shape[1])
    bf16 = jnp.bfloat16
    outs = [like(u), like(c), like(u, dtype=bf16), like(u, (cols, rows), bf16)]
    outs += [like(u, (SUBLANES, rows)), like(u, (SUBLANES, 128))]
    outs += [like(c, part), like(u, (part[0], rows), bf16), like(c, part, bf16)]
    operands = (u, c, values, coords, counts)
    return call(
        first_kernel,
        "first_chunk",
        [pltpu.with_memory_space_constraint(x, pltpu.HBM) for x in operands],
        [HBM] * 5,
        outs,
        [VMEM] * len(outs),
        scratch=[
            pltpu.VMEM(values.shape[1:], values.dtype),
            pltpu.SMEM(coords.shape, coords.dtype),
            pltpu.SMEM(counts.shape, counts.dtype),
            pltpu.SemaphoreType.DMA((6,)),
        ],
    )


def other_kernel(tile, row_half, c_ref, dense, live, residue, col_half, *c_outs):
    start, cols = c_ref.shape[0] - residue.shape[0], c_ref.shape[0]
    rest = slice(start, cols)
    residue[...], col_half[...], new = columns_step(
        start, tile, row_half[...], c_ref[rest], dense[rest], live
    )
    for at, c_out in zip(spans(EARLY, cols)[1:], c_outs):
        c_out[...] = new[at.start - start : at.stop - start]


def others(line, tile, row_half, c, laid):
    cols, rank = c.shape
    chunks = spans(EARLY, cols)[1:]
    rest = cols - chunks[0].start
    outs = [like(row_half, (rest, row_half.shape[0])), like(row_half, (rest, rank))]
    return line.call(
        functools.partial(other_kernel, tile),
        "other_chunks",
        (row_half, c, *laid),
        outs + [like(c, (size(at), rank)) for at in chunks],
    )


def layout_kernel(x_ref, coords, counts, *refs):
    outs = refs[2:]
    later = len(outs) // 2
    for s in range(later):
        scatter(s + 1, x_ref.at[s + 1], coords, counts, outs[s], outs[later + s])


def layout(line, values, coords, counts, rows, cols):
    later = values.shape[0] - 1
    outs = [like(values, (cols, rows))] * later
    outs += [like(values, (SUBLANES, rows), jnp.float32)] * later
    line.turn, *out = call(
        layout_kernel,
        "lay_out_tiles",
        (values, coords, counts, line.turn),
        [VMEM, SMEM, SMEM, VMEM],
        [like(line.turn), *outs],
        [VMEM] * (1 + len(outs)),
        aliases={3: 0},
    )
    return list(zip(out[:later], out[later:]))


def columns_kernel(at, cuts, tile, row_half, dense, live, *refs):
    *cs, c_out, residue, col_half = refs
    parts = [c[cut] for c, cut in zip(cs, cuts)]
    cols = parts[0] if len(parts) == 1 else jnp.concatenate(parts, axis=0)
    residue[...], col_half[...], c_out[...] = columns_step(
        at.start, tile, row_half[...], cols, dense[at], live
    )


def columns(line, at, weight, tile, row_half, arrived, laid):
    cs, cuts = [], []
    for there, c in arrived:
        start, stop = max(at.start, there.start), min(at.stop, there.stop)
        if start < stop:
            cs.append(c)
            cuts.append(slice(start - there.start, stop - there.start))
    rows, rank = row_half.shape
    part, bf16 = (size(at), rank), jnp.bfloat16
    return line.call(
        functools.partial(columns_kernel, at, cuts, tile),
        "columns_step",
        (row_half, *laid, *cs),
        [like(cs[0], part), like(row_half, (size(at), rows)), like(row_half, part, bf16)],
        flops=int(weight),
    )


def rows_kernel(_, __, *refs):
    *pairs, u_out, half_out = refs
    n = len(pairs) // 2
    u_new = sgd(u_out[...], rows_gradient(pairs[:n], pairs[n:]))
    u_out[...] = u_new
    half_out[...] = u_new.astype(jnp.bfloat16)


def rows(line, u, row_half, residues, halves):
    return line.call(
        rows_kernel,
        "rows_step",
        (u, row_half, *residues, *halves),
        [like(u), like(row_half)],
        aliases={0: 0, 1: 1},
    )


def gradient_kernel(*refs):
    *pairs, acc = refs
    n = len(pairs) // 2
    acc[...] = rows_gradient(pairs[:n], pairs[n:])


def last_kernel(tile, u_ref, row_half, dense, live, c_ref, acc, _, *refs):
    n = len(LATER) - 2
    done, (u_hbm, c_hbm, u_new, c_new, sems) = refs[:n], refs[n:]
    chunks = spans(LATER, c_hbm.shape[0])
    copies = []

    def copy(source, target, at):
        place = pl.ds(at, source.shape[0])
        copies.append(pltpu.make_async_copy(source, target.at[place], sems.at[len(copies)]))
        copies[-1].start()

    for h, c in enumerate(done):
        copy(c, c_hbm, chunks[h].start)
    at = chunks[n]
    residue, col_half, new_cols = columns_step(
        at.start, tile, row_half[...], c_ref[...], dense[at], live
    )
    for r in range(u_ref.shape[0] // tile):
        part = span(r, tile)
        grad = acc[part] + dot(residue[:, part], col_half, ((0,), (0,)))
        u_new[part] = sgd(u_ref[part], grad)
        copy(u_new.at[pl.ds(r * tile, tile)], u_hbm, r * tile)
    c_new[...] = new_cols
    copy(c_new, c_hbm, at.start)
    for started in copies:
        started.wait()


def final(line, tile, u, row_half, cs, laid):
    cols, rank = laid[0].shape[0], u.shape[1]
    *before, _ = spans(LATER, cols)
    n = len(before)
    steps = [
        columns(line, at, weight, tile, row_half, cs[h : h + 1], laid)
        for h, (at, weight) in enumerate(zip(before, LATER_WEIGHTS))
    ]
    done, residues, halves = zip(*steps)
    (acc,) = line.call(
        gradient_kernel,
        "rows_gradient",
        (*residues, *halves),
        [like(u)],
    )
    return call(
        functools.partial(last_kernel, tile),
        "last_columns_and_rows",
        (u, row_half, *laid, cs[n][1], acc, line.turn, *done),
        [VMEM] * (7 + n),
        [like(u), like(u, (cols, rank))],
        [HBM, HBM],
        scratch=[
            pltpu.VMEM(u.shape, u.dtype),
            pltpu.VMEM(cs[n][1].shape, u.dtype),
            pltpu.SemaphoreType.DMA((n + 1 + u.shape[0] // tile,)),
        ],
    )


def shifted(chunk, axis):
    n = lax.axis_size(axis)
    return lax.ppermute(chunk, axis, [(i, (i + 1) % n) for i in range(n)])


def per_device(row_factors, col_factors, tile_values, tile_coords, tile_counts):
    tile = tile_values.shape[2]
    strata = tile_values.shape[0]
    coords, counts = tile_coords.transpose(0, 2, 1), tile_counts.transpose(1, 0)
    sizes = row_factors.shape[0], col_factors.shape[0]
    u, c, row_half, *laid0, turn, done, residue, half = first(
        row_factors, col_factors, tile_values, coords, counts
    )
    line = Line(turn)
    cs = [shifted(done, "blk")]
    residues, halves, *done = others(line, tile, row_half, c, laid0)
    cs += [shifted(d, "blk") for d in done]
    laid = layout(line, tile_values, coords, counts, *sizes)
    u, row_half = rows(line, u, row_half, (residue, residues), (half, halves))

    cs = list(zip(spans(EARLY, sizes[1]), cs))
    for stratum in range(1, strata - 1):
        axis = "group" if stratum == 2 else "blk"
        edges, weights = (EARLY, EARLY_WEIGHTS) if stratum < 2 else (LATER, LATER_WEIGHTS)
        arrived, cs, residues, halves = cs, [], [], []
        for at, weight in zip(spans(edges, sizes[1]), weights):
            done, residue, half = columns(
                line, at, weight, tile, row_half, arrived, laid[stratum - 1]
            )
            cs.append((at, shifted(done, axis)))
            residues.append(residue)
            halves.append(half)
        u, row_half = rows(line, u, row_half, residues, halves)
    return final(line, tile, u, row_half, cs, laid[-1])


def solution(mesh):
    return jax.shard_map(
        per_device,
        mesh=mesh,
        in_specs=(
            P(("blk", "group"), None),
            P(("blk", "group"), None),
            P(None, ("blk", "group"), None, None),
            P(None, ("blk", "group"), None),
            P(None, ("blk", "group")),
        ),
        out_specs=(P(("blk", "group"), None), P(("blk", "group"), None)),
        check_vma=False,
    )
```
